128 devices in a mesh: ctx: 16 (over y, x), grp: 8 (over z, core).
Axes of the slice: x: 4, y: 4, z: 4, core: 2. Of those that a mesh axis runs over, the one named last changes fastest.
Arguments:
- queries: bfloat16 [8, 8192, 1024], P('grp', 'ctx'), may hold values from -140 to 140
- attn_keys: bfloat16 [8, 8192, 128], P('grp', 'ctx'), may hold values from -6 to 6
- attn_values: bfloat16 [8, 8192, 128], P('grp', 'ctx'), may hold values from -6 to 6
- attn_output: bfloat16 [8, 8192, 1024], P('grp', 'ctx'), may hold values from -6 to 6
- output_grad: bfloat16 [8, 8192, 1024], P('grp', 'ctx'), may hold values from -6 to 6
- chain_lens: int32 [8, 3], P('grp'), may hold values from 1 to 6144, 8192 in all within a row
Outputs:
- query_grad: bfloat16 [8, 8192, 1024], P('grp', 'ctx')
- key_grad: bfloat16 [8, 8192, 128], P('grp', 'ctx')
- value_grad: bfloat16 [8, 8192, 128], P('grp', 'ctx')
The draws below stay inside these ranges and needn't reach their ends.
Inputs may be any that keep to these rules, and one draw needn't show every extreme that they name: `chain_lens`: each row lists the 3 chain lengths of one packed batch in order; they sum to 8192 and the longest is 6144.
All inputs are finite; a program needn't handle non-finite values.
Results may differ from the reference program's by a relative error of at most 0.0049.
Values may be sent and summed in bfloat16 or wider, within the bound.
A program may use at most 128 MiB of HBM per device.

```python
import math
import jax
import jax.numpy as jnp
import numpy as np
from jax import lax

KV_GROUPS = 1
GQA = 8
HEAD_DIM = 128
BLOCK = 512
CHAINS = 3
TOKENS = 8192
GROUPS = 8
LONGEST = 6144


def shared_keys(key):
    return jnp.clip(jax.random.normal(key, (GROUPS, TOKENS, KV_GROUPS * HEAD_DIM), jnp.float32), -6.0, 6.0)


def draw_attn_keys(key, part):
    common = shared_keys(key)
    return common.astype(jnp.bfloat16)


def draw_queries(key, part):
    key = jax.random.fold_in(key, 5)
    normal_part = jnp.clip(jax.random.normal(key, (GROUPS, TOKENS, KV_GROUPS * GQA * HEAD_DIM), jnp.float32), -6.0, 6.0)
    return normal_part.astype(jnp.bfloat16)


def levels(rng, extent, pieces, smallest, top_value):
    level, own = 1.0, jax.random.fold_in(rng, 6)
    for dim, shards_of in pieces:
        heights = jnp.exp(jax.random.uniform(jax.random.fold_in(own, dim), (shards_of,), jnp.float32, smallest / len(pieces), top_value / len(pieces)))
        level = level * jnp.repeat(heights, extent[dim] // shards_of).reshape([-1 if axis == dim else 1 for axis in range(len(extent))])
    return level


def split_up(amount, total, bound, slope):
    weights = [(1 << 20) // math.isqrt(standing ** slope) + 1 for standing in range(2, amount + 1)]
    surplus, given = total - bound - (amount - 1), [1] * (amount - 1)
    while surplus > 0:
        movable = [i for i in range(amount - 1) if given[i] < bound]
        mass, budget = sum([weights[i] for i in movable]), surplus
        for i in movable:
            more = min(bound - given[i], max(1, budget * weights[i] // mass), surplus)
            given[i] = given[i] + more
            surplus = surplus - more
    return np.array([bound] + given)


def ragged_sizes(stream_key, number_of, total, most, slope):
    if number_of == 2:
        one = jax.random.randint(stream_key, (), max(1, total - most), min(most, total - 1) + 1)
        return jnp.stack([one, total - one])
    sizes = jnp.asarray(split_up(number_of, total, most, slope), jnp.int32)
    pairs = (number_of - 1) // 2
    giver, sink = sizes[1:1 + 2 * pairs:2], sizes[2:2 + 2 * pairs:2]
    room = jnp.minimum(giver - 1, most - sink)
    moved = jax.random.randint(jax.random.fold_in(stream_key, 1), (pairs,), 0, 1 << 20) % (room + 1)
    sizes = sizes.at[1:1 + 2 * pairs:2].set(giver - moved).at[2:2 + 2 * pairs:2].set(sink + moved)
    return sizes[jax.random.permutation(jax.random.fold_in(stream_key, 2), number_of)]


def centred(rng, shape, width, bound, shards=(), held_as=jnp.bfloat16):
    values = jax.random.normal(rng, shape, jnp.float32) * width
    if len(shards) > 0:
        values = levels(rng, shape, shards, -0.22, 0.18) * values
    return jnp.clip(values, min=-bound, max=bound).astype(held_as)


def setup_inputs(seed: int = 0) -> dict:
    key_of = jax.random.split(jax.random.key(seed), 7)
    queries = draw_queries(jax.random.fold_in(key_of[6], 71), 0)
    attn_keys = draw_attn_keys(jax.random.fold_in(key_of[6], 71), 0)
    attn_values = centred(key_of[2], (GROUPS, TOKENS, KV_GROUPS * HEAD_DIM), 1.0, 6.0, ((0, 8), (1, 16)))
    attn_output = centred(key_of[3], (GROUPS, TOKENS, KV_GROUPS * GQA * HEAD_DIM), 1.0, 6.0, ((0, 8), (1, 16)))
    output_grad = centred(key_of[4], (GROUPS, TOKENS, KV_GROUPS * GQA * HEAD_DIM), 1.0, 6.0, ((0, 8), (1, 16)))
    chain_lens = jax.vmap(lambda own: ragged_sizes(own, CHAINS, TOKENS, LONGEST, 2))(jax.random.split(key_of[5], GROUPS)).reshape((GROUPS, CHAINS)).astype(jnp.int32)
    return {"queries": queries, "attn_keys": attn_keys, "attn_values": attn_values, "attn_output": attn_output, "output_grad": output_grad, "chain_lens": chain_lens}


def chain_number(positions, chain_ends):
    return jnp.sum((positions[:, None] >= chain_ends[None, :]).astype(jnp.int32), axis=1)


def batch_grads(queries, attn_keys, attn_values, attn_output, output_grad, chain_lens):
    token_count = queries.shape[0]
    head_scale = HEAD_DIM ** -0.5
    chain_ends = jnp.cumsum(chain_lens).astype(jnp.int32)
    positions = jnp.arange(token_count, dtype=jnp.int32)
    chains = chain_number(positions, chain_ends)
    query_heads = queries.astype(jnp.float32).reshape(token_count, KV_GROUPS, GQA, HEAD_DIM)
    grad_heads = output_grad.astype(jnp.float32).reshape(token_count, KV_GROUPS, GQA, HEAD_DIM)
    output_heads = attn_output.astype(jnp.float32).reshape(token_count, KV_GROUPS, GQA, HEAD_DIM)
    key_heads = attn_keys.astype(jnp.float32).reshape(token_count, KV_GROUPS, HEAD_DIM)
    value_heads = attn_values.astype(jnp.float32).reshape(token_count, KV_GROUPS, HEAD_DIM)
    key_total = jnp.zeros((token_count, KV_GROUPS, HEAD_DIM), jnp.float32)
    value_total = jnp.zeros((token_count, KV_GROUPS, HEAD_DIM), jnp.float32)
    query_blocks = []
    for block_number in range(token_count // BLOCK):
        first_row = block_number * BLOCK
        last_row = first_row + BLOCK
        query_rows = query_heads[first_row:last_row]
        grad_rows = grad_heads[first_row:last_row]
        output_rows = output_heads[first_row:last_row]
        scores = jnp.einsum("pjrd,sjd->jrps", query_rows, key_heads[:last_row]) * head_scale
        allowed = (chains[:last_row][None, :] == chains[first_row:last_row][:, None]) & (positions[:last_row][None, :] <= positions[first_row:last_row][:, None])
        masked = jnp.where(allowed, scores, -jnp.inf)
        best_score = jnp.max(masked, axis=-1)
        log_total = best_score + jnp.log(jnp.sum(jnp.exp(masked - best_score[..., None]), axis=-1))
        attn_probs = jnp.exp(masked - log_total[..., None])
        row_delta = jnp.einsum("pjrd,pjrd->jrp", grad_rows, output_rows)
        dprobs = jnp.einsum("pjrd,sjd->jrps", grad_rows, value_heads[:last_row])
        dscores = attn_probs * (dprobs - row_delta[..., None])
        probs_half = lax.optimization_barrier(attn_probs.astype(jnp.bfloat16)).astype(jnp.float32)
        dscores_half = lax.optimization_barrier(dscores.astype(jnp.bfloat16)).astype(jnp.float32)
        value_total = value_total.at[:last_row].add(jnp.einsum("jrps,pjrd->sjd", probs_half, grad_rows))
        key_total = key_total.at[:last_row].add(jnp.einsum("jrps,pjrd->sjd", dscores_half, query_rows) * head_scale)
        query_block = jnp.einsum("jrps,sjd->pjrd", dscores_half, key_heads[:last_row]) * head_scale
        query_blocks.append(query_block.reshape(BLOCK, -1).astype(jnp.bfloat16))
    query_grad = jnp.concatenate(query_blocks, axis=0)
    key_grad = key_total.reshape(token_count, -1).astype(jnp.bfloat16)
    value_grad = value_total.reshape(token_count, -1).astype(jnp.bfloat16)
    return query_grad, key_grad, value_grad


def reference(queries, attn_keys, attn_values, attn_output, output_grad, chain_lens):
    query_grad, key_grad, value_grad = lax.map(lambda group_items: batch_grads(*group_items), (queries, attn_keys, attn_values, attn_output, output_grad, chain_lens))
    return (query_grad, key_grad, value_grad)
```

```python
import functools, math
import jax, jax.numpy as jnp
from jax import lax
from jax.experimental import pallas as pl
from jax.experimental.pallas import tpu as pltpu
from jax.sharding import PartitionSpec as P

HD = 128; GQA = 8
TP = 32
R = TP * GQA
SCALE = HD ** -0.5
C2 = SCALE * math.log2(math.e)
NT = (((1,), (1,)), ((), ()))
NN = (((1,), (0,)), ((), ()))

def dot(a, b, dims):
    return lax.dot_general(a, b, dims, preferred_element_type=jnp.float32)

def kernel(BIG, base_ref, ends_ref, q_ref, do_ref, delta_ref, k_ref, v_ref, dq_ref, dk_ref, dv_ref,
           kt, pbuf, mbuf, dka, dva, qs, dos, dqt):
    T = k_ref.shape[0]
    SUB = 128
    def init(i, _):
        rows = pl.ds(pl.multiple_of(i * 512, 512), 512)
        kt[:, rows] = k_ref[rows, :].T
        dka[rows, :] = jnp.zeros((512, HD), jnp.float32)
        dva[rows, :] = jnp.zeros((512, HD), jnp.float32)
        return 0
    lax.fori_loop(0, T // 512, init, 0)
    e0 = ends_ref[0]; e1 = ends_ref[1]

    def tile(t, _):
        p0 = base_ref[t]
        cs = jnp.where(p0 < e0, 0, jnp.where(p0 < e1, e0, e1))
        lo = (cs // SUB) * SUB
        hi = ((p0 + TP + SUB - 1) // SUB) * SUB
        nb = (hi - lo) // BIG
        nr = ((hi - lo) - nb * BIG) // SUB
        for h in range(GQA):
            qs[h * TP:(h + 1) * TP, :] = q_ref[t, :, h * HD:(h + 1) * HD]
            dos[h * TP:(h + 1) * TP, :] = do_ref[t, :, h * HD:(h + 1) * HD]
        lane = lax.broadcasted_iota(jnp.int32, (1, R), 1)
        rpos = p0 + lane % TP
        rstart = jnp.where(rpos < e0, 0, jnp.where(rpos < e1, e0, e1))

        def stats(first, size, slot, masked, carry):
            m, l = carry
            first = pl.multiple_of(first, SUB)
            s = dot(k_ref[pl.ds(first, size), :], qs[...], NT)
            if masked:
                spos = first + lax.broadcasted_iota(jnp.int32, (size, 1), 0)
                s = jnp.where((spos >= rstart) & (spos <= rpos), s, -1e30)
            mn = jnp.maximum(m, jnp.max(s, axis=0, keepdims=True))
            p = jnp.exp2((s - mn) * C2)
            pbuf[pl.ds(first, size), :] = p
            mbuf[slot] = mn
            l = l * jnp.exp2((m - mn) * C2) + jnp.sum(p, axis=0, keepdims=True)
            return mn, l

        carry = (jnp.full((1, R), -1e30, jnp.float32), jnp.zeros((1, R), jnp.float32))
        safe_lo = rstart_max = jnp.where(p0 + TP - 1 < e0, 0, jnp.where(p0 + TP - 1 < e1, e0, e1))
        def sb(j, c):
            first = lo + j * BIG
            need = (first < rstart_max) | (first + BIG - 1 > p0)
            return lax.cond(need, lambda c: stats(first, BIG, j, True, c), lambda c: stats(first, BIG, j, False, c), c)
        carry = lax.fori_loop(0, nb, sb, carry)
        def sr(j, c):
            return stats(lo + nb * BIG + j * SUB, SUB, nb + j, True, c)
        m, l = lax.fori_loop(0, nr, sr, carry)
        linv = 1.0 / l
        delta = delta_ref[t]
        dqt[...] = jnp.zeros((HD, R), jnp.float32)

        def grads(first, size, slot):
            first = pl.multiple_of(first, SUB)
            rows = pl.ds(first, size)
            f = jnp.exp2((mbuf[slot] - m) * C2) * linv
            p = pbuf[rows, :] * f
            dp = dot(v_ref[rows, :], dos[...], NT)
            ds = (p * (dp - delta)).astype(jnp.bfloat16)
            dva[rows, :] += dot(p.astype(jnp.bfloat16), dos[...], NN)
            dka[rows, :] += dot(ds, qs[...], NN)
            dqt[...] += dot(kt[:, rows], ds, NN)
        def gb(j, _):
            grads(lo + j * BIG, BIG, j)
            return 0
        lax.fori_loop(0, nb, gb, 0)
        def gr(j, _):
            grads(lo + nb * BIG + j * SUB, SUB, nb + j)
            return 0
        lax.fori_loop(0, nr, gr, 0)
        dq = (dqt[...].T * SCALE).astype(jnp.bfloat16)
        for h in range(GQA):
            dq_ref[t, :, h * HD:(h + 1) * HD] = dq[h * TP:(h + 1) * TP, :]
        return 0
    lax.fori_loop(0, q_ref.shape[0], tile, 0)
    def fin(i, _):
        rows = pl.ds(pl.multiple_of(i * 512, 512), 512)
        dk_ref[rows, :] = (dka[rows, :] * SCALE).astype(dk_ref.dtype)
        dv_ref[rows, :] = dva[rows, :].astype(dv_ref.dtype)
        return 0
    lax.fori_loop(0, T // 512, fin, 0)

def call(base, ends, q, do, delta, k, v, out_dt=jnp.bfloat16, BIG=512):
    T = k.shape[0]; n = q.shape[0]
    vm = pl.BlockSpec(memory_space=pltpu.VMEM); sm = pl.BlockSpec(memory_space=pltpu.SMEM)
    return pl.pallas_call(
        functools.partial(kernel, BIG),
        out_shape=(jax.ShapeDtypeStruct(q.shape, jnp.bfloat16), jax.ShapeDtypeStruct((T, HD), out_dt), jax.ShapeDtypeStruct((T, HD), out_dt)),
        in_specs=[sm, sm, vm, vm, vm, vm, vm], out_specs=(vm, vm, vm),
        scratch_shapes=[pltpu.VMEM((HD, T), jnp.bfloat16), pltpu.VMEM((T, R), jnp.float32), pltpu.VMEM((T // BIG + BIG // 128 + 1, 1, R), jnp.float32),
            pltpu.VMEM((T, HD), jnp.float32), pltpu.VMEM((T, HD), jnp.float32), pltpu.VMEM((R, HD), jnp.bfloat16), pltpu.VMEM((R, HD), jnp.bfloat16), pltpu.VMEM((HD, R), jnp.float32)],
        compiler_params=pltpu.CompilerParams(vmem_limit_bytes=56 * 2**20),
    )(base, ends, q, do, delta, k, v)


def on_device(queries, attn_keys, attn_values, attn_output, output_grad, chain_lens):
    n = lax.axis_size("ctx")
    me = lax.axis_index("ctx")
    odd = me % 2 == 1
    ends = jnp.cumsum(chain_lens[0]).astype(jnp.int32)
    k = lax.all_gather(attn_keys[0], "ctx", axis=0, tiled=True)
    v = lax.all_gather(attn_values[0], "ctx", axis=0, tiled=True)
    order = lambda x: jnp.where(odd, x[::-1], x)
    delta = jnp.einsum(
        "tphd,tphd->thp",
        output_grad[0].reshape(n, TP, GQA, HD),
        attn_output[0].reshape(n, TP, GQA, HD),
        preferred_element_type=jnp.float32,
    ).reshape(n, 1, R)
    rows = jnp.stack([queries[0].reshape(n, TP, -1), output_grad[0].reshape(n, TP, -1)], 1)
    rows = lax.all_to_all(order(rows), "ctx", 0, 0)
    delta = lax.all_to_all(order(delta), "ctx", 0, 0)
    block = jnp.arange(n, dtype=jnp.int32)
    base = block * (n * TP) + TP * jnp.where(block % 2 == 0, me, n - 1 - me)
    dq, dk, dv = call(base, ends, rows[:, 0], rows[:, 1], delta, k, v, jnp.float32, 1024)
    dq = order(lax.all_to_all(dq, "ctx", 0, 0)).reshape(1, n * TP, -1)
    dk = lax.psum_scatter(dk, "ctx", scatter_dimension=0, tiled=True)
    dv = lax.psum_scatter(dv, "ctx", scatter_dimension=0, tiled=True)
    return dq, dk.astype(jnp.bfloat16)[None], dv.astype(jnp.bfloat16)[None]


def solution(mesh):
    tok = P("grp", "ctx", None)
    return jax.shard_map(
        on_device,
        mesh=mesh,
        in_specs=(tok, tok, tok, tok, tok, P("grp", None)),
        out_specs=(tok, tok, tok),
        check_vma=False,
    )
```

```python
import functools, math
import jax, jax.numpy as jnp
from jax import lax
from jax.experimental import pallas as pl
from jax.experimental.pallas import tpu as pltpu
from jax.sharding import PartitionSpec as P

HD = 128; GQA = 8
BLOCK = 512
TP = 32
R = TP * GQA
SCALE = HD ** -0.5
C2 = SCALE * math.log2(math.e)
NT = (((1,), (1,)), ((), ()))
NN = (((1,), (0,)), ((), ()))

def dot(a, b, dims):
    return lax.dot_general(a, b, dims, preferred_element_type=jnp.float32)

def kernel(BIG, base_ref, ends_ref, q_ref, do_ref, delta_ref, k_ref, v_ref, dq_ref, dk_ref, dv_ref,
           kt, pbuf, mbuf, dka, dva, qs, dos, dqt):
    T = k_ref.shape[0]
    SUB = 128
    def init(i, _):
        rows = pl.ds(pl.multiple_of(i * 512, 512), 512)
        kt[:, rows] = k_ref[rows, :].T
        dka[rows, :] = jnp.zeros((512, HD), jnp.float32)
        dva[rows, :] = jnp.zeros((512, HD), jnp.float32)
        return 0
    lax.fori_loop(0, T // 512, init, 0)
    e0 = ends_ref[0]; e1 = ends_ref[1]

    def tile(t, _):
        p0 = base_ref[t]
        cs = jnp.where(p0 < e0, 0, jnp.where(p0 < e1, e0, e1))
        lo = (cs // SUB) * SUB
        hi = ((p0 + TP + SUB - 1) // SUB) * SUB
        nb = (hi - lo) // BIG
        nr = ((hi - lo) - nb * BIG) // SUB
        for h in range(GQA):
            qs[h * TP:(h + 1) * TP, :] = q_ref[t, :, h * HD:(h + 1) * HD]
            dos[h * TP:(h + 1) * TP, :] = do_ref[t, :, h * HD:(h + 1) * HD]
        lane = lax.broadcasted_iota(jnp.int32, (1, R), 1)
        rpos = p0 + lane % TP
        rstart = jnp.where(rpos < e0, 0, jnp.where(rpos < e1, e0, e1))

        def stats(first, size, slot, masked, carry):
            m, l = carry
            first = pl.multiple_of(first, SUB)
            s = dot(k_ref[pl.ds(first, size), :], qs[...], NT)
            if masked:
                spos = first + lax.broadcasted_iota(jnp.int32, (size, 1), 0)
                s = jnp.where((spos >= rstart) & (spos <= rpos), s, -1e30)
            mn = jnp.maximum(m, jnp.max(s, axis=0, keepdims=True))
            p = jnp.exp2((s - mn) * C2)
            pbuf[pl.ds(first, size), :] = p
            mbuf[slot] = mn
            l = l * jnp.exp2((m - mn) * C2) + jnp.sum(p, axis=0, keepdims=True)
            return mn, l

        carry = (jnp.full((1, R), -1e30, jnp.float32), jnp.zeros((1, R), jnp.float32))
        safe_lo = rstart_max = jnp.where(p0 + TP - 1 < e0, 0, jnp.where(p0 + TP - 1 < e1, e0, e1))
        def sb(j, c):
            first = lo + j * BIG
            need = (first < rstart_max) | (first + BIG - 1 > p0)
            return lax.cond(need, lambda c: stats(first, BIG, j, True, c), lambda c: stats(first, BIG, j, False, c), c)
        carry = lax.fori_loop(0, nb, sb, carry)
        def sr(j, c):
            return stats(lo + nb * BIG + j * SUB, SUB, nb + j, True, c)
        m, l = lax.fori_loop(0, nr, sr, carry)
        linv = 1.0 / l
        delta = delta_ref[t, 0:1, :]
        dqt[...] = jnp.zeros((HD, R), jnp.float32)

        def grads(first, size, slot):
            first = pl.multiple_of(first, SUB)
            rows = pl.ds(first, size)
            f = jnp.exp2((mbuf[slot] - m) * C2) * linv
            p = pbuf[rows, :] * f
            dp = dot(v_ref[rows, :], dos[...], NT)
            ds = (p * (dp - delta)).astype(jnp.bfloat16)
            dva[rows, :] += dot(p.astype(jnp.bfloat16), dos[...], NN)
            dka[rows, :] += dot(ds, qs[...], NN)
            dqt[...] += dot(kt[:, rows], ds, NN)
        def gb(j, _):
            grads(lo + j * BIG, BIG, j)
            return 0
        lax.fori_loop(0, nb, gb, 0)
        def gr(j, _):
            grads(lo + nb * BIG + j * SUB, SUB, nb + j)
            return 0
        lax.fori_loop(0, nr, gr, 0)
        dq = (dqt[...].T * SCALE).astype(jnp.bfloat16)
        for h in range(GQA):
            dq_ref[t, :, h * HD:(h + 1) * HD] = dq[h * TP:(h + 1) * TP, :]
        return 0
    lax.fori_loop(0, q_ref.shape[0], tile, 0)
    def fin(i, _):
        rows = pl.ds(pl.multiple_of(i * 512, 512), 512)
        dk_ref[rows, :] = (dka[rows, :] * SCALE).astype(dk_ref.dtype)
        dv_ref[rows, :] = dva[rows, :].astype(dv_ref.dtype)
        return 0
    lax.fori_loop(0, T // 512, fin, 0)

def call(base, ends, q, do, delta, k, v, out_dt=jnp.bfloat16, BIG=512):
    T = k.shape[0]; n = q.shape[0]
    vm = pl.BlockSpec(memory_space=pltpu.VMEM); sm = pl.BlockSpec(memory_space=pltpu.SMEM)
    return pl.pallas_call(
        functools.partial(kernel, BIG),
        out_shape=(jax.ShapeDtypeStruct(q.shape, jnp.bfloat16), jax.ShapeDtypeStruct((T, HD), out_dt), jax.ShapeDtypeStruct((T, HD), out_dt)),
        in_specs=[sm, sm, vm, vm, vm, vm, vm], out_specs=(vm, vm, vm),
        scratch_shapes=[pltpu.VMEM((HD, T), jnp.bfloat16), pltpu.VMEM((T, R), jnp.float32), pltpu.VMEM((T // BIG + BIG // 128 + 1, 1, R), jnp.float32),
            pltpu.VMEM((T, HD), jnp.float32), pltpu.VMEM((T, HD), jnp.float32), pltpu.VMEM((R, HD), jnp.bfloat16), pltpu.VMEM((R, HD), jnp.bfloat16), pltpu.VMEM((HD, R), jnp.float32)],
        compiler_params=pltpu.CompilerParams(vmem_limit_bytes=56 * 2**20),
    )(base, ends, q, do, delta, k, v)


MESH = pl.DeviceIdType.MESH
SIDE = 4
SENDERS = SIDE * SIDE


def greet(me):
    barrier = pltpu.get_barrier_semaphore()
    for step in range(1, SENDERS):
        pl.semaphore_signal(barrier, inc=1, device_id={"ctx": (me + step) % SENDERS}, device_id_type=MESH)
    pl.semaphore_wait(barrier, SENDERS - 1)


def gather_kernel(k_ref, v_ref, q_ref, do_ref, de_ref, k_all, v_all, q_out, do_out, de_out, kv_send, kv_recv, row_send, row_recv, own_sem):
    me = lax.axis_index("ctx")
    y, x = me // SIDE, me % SIDE
    greet(me)

    def block(ref, i):
        return ref.at[pl.ds(pl.multiple_of(i * BLOCK, BLOCK), BLOCK)]

    def kv_copy(which, src, owner, to, slot):
        whole = (k_all, v_all)[which]
        return pltpu.make_async_remote_copy(
            src_ref=src, dst_ref=block(whole, owner), send_sem=kv_send.at[which, slot], recv_sem=kv_recv.at[which, owner],
            device_id={"ctx": to}, device_id_type=MESH)

    x_peers = [y * SIDE + (x + s) % SIDE for s in (1, 3, 2)]
    y_peers = [((y + s) % SIDE) * SIDE + x for s in (1, 3, 2)]
    own = [pltpu.make_async_copy(k_ref, block(k_all, me), own_sem.at[0]), pltpu.make_async_copy(v_ref, block(v_all, me), own_sem.at[1])]
    sends = []
    for which, ref in ((0, k_ref), (1, v_ref)):
        first, second = ((x_peers, y_peers), (y_peers, x_peers))[which]
        for n, to in enumerate(first + second):
            sends.append(kv_copy(which, ref, me, to, n))
    for c in sends:
        c.start()
    for c in own:
        c.start()

    def chunk_of(block_at, dev):
        return jnp.where(block_at % 2 == 0, dev, SENDERS - 1 - dev)

    row_copies = []
    for step in range(1, SENDERS):
        to = (me + step) % SENDERS
        c = chunk_of(me, to)
        for n, (src, dst) in enumerate(((q_ref, q_out), (do_ref, do_out), (de_ref, de_out))):
            row_copies.append(pltpu.make_async_remote_copy(
                src_ref=src.at[c], dst_ref=dst.at[me], send_sem=row_send.at[n, step], recv_sem=row_recv.at[n, me],
                device_id={"ctx": to}, device_id_type=MESH))
    for c in row_copies:
        c.start()
    c = chunk_of(me, me)
    for n, (src, dst) in enumerate(((q_ref, q_out), (do_ref, do_out), (de_ref, de_out))):
        own.append(pltpu.make_async_copy(src.at[c], dst.at[me], own_sem.at[2 + n]))
        own[-1].start()

    def arrived(which, owner):
        kv_copy(which, block((k_all, v_all)[which], owner), owner, me, 0).wait_recv()

    for n in range(3):
        for which in (0, 1):
            first, second = ((x_peers, y_peers), (y_peers, x_peers))[which]
            owner = first[n]
            arrived(which, owner)
            for m, to in enumerate(second):
                c = kv_copy(which, block((k_all, v_all)[which], owner), owner, to, 6 + 3 * n + m)
                c.start()
                sends.append(c)
    for which in (0, 1):
        for s in range(1, SIDE):
            for r in range(SIDE):
                if which == 0:
                    arrived(which, ((y + s) % SIDE) * SIDE + (x + r) % SIDE)
                else:
                    arrived(which, ((y + r) % SIDE) * SIDE + (x + s) % SIDE)
    for step in range(1, SENDERS):
        source = (me + step) % SENDERS
        for n, (src, dst) in enumerate(((q_ref, q_out), (do_ref, do_out), (de_ref, de_out))):
            pltpu.make_async_remote_copy(
                src_ref=src.at[0], dst_ref=dst.at[source], send_sem=row_send.at[n, 0], recv_sem=row_recv.at[n, source],
                device_id={"ctx": me}, device_id_type=MESH).wait_recv()
    for c in sends + row_copies:
        c.wait_send()
    for c in own:
        c.wait()


def gather(k, v, q, do, de):
    anyspace = pl.BlockSpec(memory_space=pl.ANY)
    T = k.shape[0] * SENDERS
    sds = jax.ShapeDtypeStruct
    dma = pltpu.SemaphoreType.DMA
    return pl.pallas_call(
        gather_kernel,
        out_shape=(sds((T, HD), k.dtype), sds((T, HD), k.dtype), sds(q.shape, q.dtype), sds(do.shape, do.dtype), sds(de.shape, de.dtype)),
        in_specs=[anyspace] * 5, out_specs=(anyspace,) * 5,
        scratch_shapes=[dma((2, 15)), dma((2, SENDERS)), dma((3, SENDERS)), dma((3, SENDERS)), dma((5,))],
        compiler_params=pltpu.CompilerParams(collective_id=0, has_side_effects=True),
    )(k, v, q, do, de)


def reduce_kernel(dk_ref, dv_ref, dq_ref, dk_out, dv_out, dq_out, own, got, mid, mid_got, send1, recv1, send2, recv2, row_send, row_recv, own_sem):
    me = lax.axis_index("ctx")
    y, x = me // SIDE, me % SIDE
    greet(me)
    steps = (1, 3, 2)

    def lane_of(which):
        return (y, x) if which == 0 else (x, y)

    def peer(which, leg, s):
        along_y = (which == 0) == (leg == 0)
        return ((y + s) % SIDE) * SIDE + x if along_y else y * SIDE + (x + s) % SIDE

    def part(ref, which, at):
        return ref.at[at] if which == 0 else ref.at[:, at]

    copies, local = [], []
    for n, s in enumerate(steps):
        for which, ref in ((0, dk_ref), (1, dv_ref)):
            at = (lane_of(which)[0] + s) % SIDE
            copies.append(pltpu.make_async_remote_copy(
                src_ref=part(ref, which, at), dst_ref=got.at[which, n], send_sem=send1.at[which, n], recv_sem=recv1.at[which, n],
                device_id={"ctx": peer(which, 0, s)}, device_id_type=MESH))
            copies[-1].start()
    for which, ref in ((0, dk_ref), (1, dv_ref)):
        local.append(pltpu.make_async_copy(part(ref, which, lane_of(which)[0]), own.at[which], own_sem.at[which]))
        local[-1].start()

    def chunk_of(block_at, dev):
        return jnp.where(block_at % 2 == 0, dev, SENDERS - 1 - dev)

    rows = []
    for step in range(1, SENDERS):
        to = (me + step) % SENDERS
        rows.append(pltpu.make_async_remote_copy(
            src_ref=dq_ref.at[to], dst_ref=dq_out.at[chunk_of(to, me)], send_sem=row_send.at[step], recv_sem=row_recv.at[chunk_of(to, me)],
            device_id={"ctx": to}, device_id_type=MESH))
        rows[-1].start()
    own_row = pltpu.make_async_copy(dq_ref.at[me], dq_out.at[chunk_of(me, me)], own_sem.at[2])
    own_row.start()

    late = []
    for which in (0, 1):
        local[which].wait()
        for n in range(3):
            pltpu.make_async_remote_copy(
                src_ref=own.at[which], dst_ref=got.at[which, n], send_sem=send1.at[which, n], recv_sem=recv1.at[which, n],
                device_id={"ctx": me}, device_id_type=MESH).wait_recv()

        def add(i, _, which=which):
            r = pl.ds(pl.multiple_of(i * 128, 128), 128)
            for b in range(SIDE):
                total = own[which, b, r, :].astype(jnp.float32)
                for n in range(3):
                    total = total + got[which, n, b, r, :].astype(jnp.float32)
                mid[which, b, r, :] = total.astype(jnp.bfloat16)
            return 0
        lax.fori_loop(0, BLOCK // 128, add, 0)
        for n, s in enumerate(steps):
            at = (lane_of(which)[1] + s) % SIDE
            late.append(pltpu.make_async_remote_copy(
                src_ref=mid.at[which, at], dst_ref=mid_got.at[which, n], send_sem=send2.at[which, n], recv_sem=recv2.at[which, n],
                device_id={"ctx": peer(which, 1, s)}, device_id_type=MESH))
            late[-1].start()
    for which, ref in ((0, dk_out), (1, dv_out)):
        for n in range(3):
            pltpu.make_async_remote_copy(
                src_ref=mid.at[which, 0], dst_ref=mid_got.at[which, n], send_sem=send2.at[which, n], recv_sem=recv2.at[which, n],
                device_id={"ctx": me}, device_id_type=MESH).wait_recv()

        def last(i, _, which=which, ref=ref):
            r = pl.ds(pl.multiple_of(i * 128, 128), 128)
            total = mid[which, lane_of(which)[1], r, :].astype(jnp.float32)
            for n in range(3):
                total = total + mid_got[which, n, r, :].astype(jnp.float32)
            ref[r, :] = total.astype(jnp.bfloat16)
            return 0
        lax.fori_loop(0, BLOCK // 128, last, 0)
    for step in range(1, SENDERS):
        c = chunk_of(me, (me + step) % SENDERS)
        pltpu.make_async_remote_copy(
            src_ref=dq_ref.at[0], dst_ref=dq_out.at[c], send_sem=row_send.at[0], recv_sem=row_recv.at[c],
            device_id={"ctx": me}, device_id_type=MESH).wait_recv()
    own_row.wait()
    for c in copies + late + rows:
        c.wait_send()


def reduce(dk, dv, dq):
    anyspace = pl.BlockSpec(memory_space=pl.ANY)
    vm = pl.BlockSpec(memory_space=pltpu.VMEM)
    sds = jax.ShapeDtypeStruct
    dma = pltpu.SemaphoreType.DMA
    bf = jnp.bfloat16
    shape = (SIDE, SIDE, BLOCK, HD)
    return pl.pallas_call(
        reduce_kernel,
        out_shape=(sds((BLOCK, HD), bf), sds((BLOCK, HD), bf), sds(dq.shape, bf)),
        in_specs=[anyspace] * 3, out_specs=(vm, vm, anyspace),
        scratch_shapes=[pltpu.VMEM((2, SIDE, BLOCK, HD), bf), pltpu.VMEM((2, 3, SIDE, BLOCK, HD), bf), pltpu.VMEM((2, SIDE, BLOCK, HD), bf),
            pltpu.VMEM((2, 3, BLOCK, HD), bf), dma((2, 3)), dma((2, 3)), dma((2, 3)), dma((2, 3)), dma((SENDERS,)), dma((SENDERS,)), dma((3,))],
        compiler_params=pltpu.CompilerParams(collective_id=1, has_side_effects=True, vmem_limit_bytes=32 * 2**20),
    )(dk.reshape(shape), dv.reshape(shape), dq)


def on_device(queries, attn_keys, attn_values, attn_output, output_grad, chain_lens):
    n = lax.axis_size("ctx")
    me = lax.axis_index("ctx")
    ends = jnp.cumsum(chain_lens[0]).astype(jnp.int32)
    delta = jnp.einsum(
        "tphd,tphd->thp",
        output_grad[0].reshape(n, TP, GQA, HD),
        attn_output[0].reshape(n, TP, GQA, HD),
        preferred_element_type=jnp.float32,
    ).reshape(n, 1, R)
    k, v, q, do, delta = gather(
        attn_keys[0],
        attn_values[0],
        queries[0].reshape(n, TP, -1),
        output_grad[0].reshape(n, TP, -1),
        jnp.broadcast_to(delta, (n, 8, R)),
    )
    block = jnp.arange(n, dtype=jnp.int32)
    base = block * (n * TP) + TP * jnp.where(block % 2 == 0, me, n - 1 - me)
    dq, dk, dv = call(base, ends, q, do, delta, k, v)
    dk, dv, dq = reduce(dk, dv, dq)
    return dq.reshape(1, n * TP, -1), dk[None], dv[None]


def solution(mesh):
    tok = P("grp", "ctx", None)
    return jax.shard_map(
        on_device,
        mesh=mesh,
        in_specs=(tok, tok, tok, tok, tok, P("grp", None)),
        out_specs=(tok, tok, tok),
        check_vma=False,
    )
```

```python
import functools, math
import jax, jax.numpy as jnp
from jax import lax
from jax.experimental import pallas as pl
from jax.experimental.pallas import tpu as pltpu
from jax.sharding import PartitionSpec as P

HD = 128
GQA = 8
BLOCK = 512
TP = 64
R = TP * GQA
SUB = 128
SB = 64
BIG = 1024
SCALE = HD ** -0.5
C2 = SCALE * math.log2(math.e)
NN = (((1,), (0,)), ((), ()))


def dot(a, b):
    return lax.dot_general(a, b, NN, preferred_element_type=jnp.float32)


def kernel(base_ref, ends_ref, q_ref, do_ref, delta_ref, k_ref, v_ref, dq_ref, dk_ref, dv_ref,
           kt, pbuf, mbuf, mrun, lrun, dka, dva, qs, dos, dqt, qst, dost):
    T = k_ref.shape[0]

    def init(i, _):
        rows = pl.ds(pl.multiple_of(i * 512, 512), 512)
        kt[:, rows] = k_ref[rows, :].T
        dka[rows, :] = jnp.zeros((512, HD), jnp.float32)
        dva[rows, :] = jnp.zeros((512, HD), jnp.float32)
        return 0
    lax.fori_loop(0, T // 512, init, 0)
    e0 = ends_ref[0]
    e1 = ends_ref[1]

    def start_of(p):
        return jnp.where(p < e0, 0, jnp.where(p < e1, e0, e1))

    def tile(t, _):
        p0 = base_ref[t]
        lo = (start_of(p0) // SUB) * SUB
        hi = ((p0 + TP + SUB - 1) // SUB) * SUB
        nb = (hi - lo) // BIG
        rest = (hi - lo) - nb * BIG
        for h in range(GQA):
            qs[h * TP:(h + 1) * TP, :] = q_ref[t, :, h * HD:(h + 1) * HD]
            dos[h * TP:(h + 1) * TP, :] = do_ref[t, :, h * HD:(h + 1) * HD]
        qst[...] = qs[...].T
        dost[...] = dos[...].T
        rpos = p0 + lax.broadcasted_iota(jnp.int32, (1, R), 1) % TP
        rstart = start_of(rpos)
        last_start = start_of(p0 + TP - 1)

        def stats(first, size, masked):
            first = pl.multiple_of(first, SUB)
            s = dot(k_ref[pl.ds(first, size), :], qst[...])
            if masked:
                spos = first + lax.broadcasted_iota(jnp.int32, (size, 1), 0)
                s = jnp.where((spos >= rstart) & (spos <= rpos), s, -1e30)
            s = s.reshape(size // SB, SB // 8, 8, R)
            m = jnp.max(s, axis=1)
            p = jnp.exp2((s - m[:, None]) * C2)
            pbuf[pl.ds(first, size), :] = p.reshape(size, R)
            mbuf[pl.ds(first // SB, size // SB)] = m
            old = mrun[...]
            new = jnp.maximum(old, jnp.max(m, axis=0))
            lrun[...] = lrun[...] * jnp.exp2((old - new) * C2) + jnp.sum(jnp.sum(p, axis=1) * jnp.exp2((m - new) * C2), axis=0)
            mrun[...] = new

        def grads(first, size):
            first = pl.multiple_of(first, SUB)
            rows = pl.ds(first, size)
            f = jnp.exp2((mbuf[pl.ds(first // SB, size // SB)] - top) * C2) * linv
            p = (pbuf[rows, :].reshape(size // SB, SB // 8, 8, R) * f[:, None]).reshape(size, R)
            dp = dot(v_ref[rows, :], dost[...])
            ds = (p * (dp - delta)).astype(jnp.bfloat16)
            dva[rows, :] += dot(p.astype(jnp.bfloat16), dos[...])
            dka[rows, :] += dot(ds, qs[...])
            dqt[...] += dot(kt[:, rows], ds)

        def sweep(body):
            def big(j, _):
                body(lo + j * BIG, BIG)
                return 0
            lax.fori_loop(0, nb, big, 0)
            at = lo + nb * BIG
            size = BIG // 2
            while size >= SUB:
                has = (rest & size) != 0
                pl.when(has)(functools.partial(body, at, size))
                at = at + jnp.where(has, size, 0)
                size //= 2

        def stats_any(first, size):
            need = (first < last_start) | (first + size - 1 > p0)
            pl.when(need)(lambda: stats(first, size, True))
            pl.when(jnp.logical_not(need))(lambda: stats(first, size, False))
        mrun[...] = jnp.full((8, R), -1e30, jnp.float32)
        lrun[...] = jnp.zeros((8, R), jnp.float32)
        sweep(stats_any)
        top = jnp.max(mrun[...], axis=0, keepdims=True)
        linv = 1.0 / jnp.sum(lrun[...] * jnp.exp2((mrun[...] - top) * C2), axis=0, keepdims=True)
        delta = delta_ref[t, 0:1, :]
        dqt[...] = jnp.zeros((HD, R), jnp.float32)
        sweep(grads)
        dq = (dqt[...].T * SCALE).astype(jnp.bfloat16)
        for h in range(GQA):
            dq_ref[t, :, h * HD:(h + 1) * HD] = dq[h * TP:(h + 1) * TP, :]
        return 0
    lax.fori_loop(0, q_ref.shape[0], tile, 0)

    def fin(i, _):
        rows = pl.ds(pl.multiple_of(i * 512, 512), 512)
        dk_ref[rows, :] = (dka[rows, :] * SCALE).astype(dk_ref.dtype)
        dv_ref[rows, :] = dva[rows, :].astype(dv_ref.dtype)
        return 0
    lax.fori_loop(0, T // 512, fin, 0)


def call(base, ends, q, do, delta, k, v):
    T = k.shape[0]
    vm = pl.BlockSpec(memory_space=pltpu.VMEM)
    sm = pl.BlockSpec(memory_space=pltpu.SMEM)
    f32 = jnp.float32
    bf = jnp.bfloat16
    return pl.pallas_call(
        kernel,
        out_shape=(jax.ShapeDtypeStruct(q.shape, bf), jax.ShapeDtypeStruct((T, HD), bf), jax.ShapeDtypeStruct((T, HD), bf)),
        in_specs=[sm, sm, vm, vm, vm, vm, vm],
        out_specs=(vm, vm, vm),
        scratch_shapes=[pltpu.VMEM((HD, T), bf), pltpu.VMEM((T, R), f32), pltpu.VMEM((T // SB, 8, R), f32), pltpu.VMEM((8, R), f32), pltpu.VMEM((8, R), f32),
            pltpu.VMEM((T, HD), f32), pltpu.VMEM((T, HD), f32), pltpu.VMEM((R, HD), bf), pltpu.VMEM((R, HD), bf), pltpu.VMEM((HD, R), f32),
            pltpu.VMEM((HD, R), bf), pltpu.VMEM((HD, R), bf)],
        compiler_params=pltpu.CompilerParams(vmem_limit_bytes=60 * 2**20),
    )(base, ends, q, do, delta, k, v)


MESH = pl.DeviceIdType.MESH
SIDE = 4
SENDERS = SIDE * SIDE
CHUNKS = 8


def source_of(dev, r):
    at = jnp.where(r % 2 == 0, dev, SENDERS - 1 - dev)
    return 2 * r + at // CHUNKS, at % CHUNKS


def taker_of(owner, c):
    at = (owner % 2) * CHUNKS + c
    return jnp.where((owner // 2) % 2 == 0, at, SENDERS - 1 - at)


def greet(me):
    barrier = pltpu.get_barrier_semaphore()
    for step in range(1, SENDERS):
        pl.semaphore_signal(barrier, inc=1, device_id={"ctx": (me + step) % SENDERS}, device_id_type=MESH)
    pl.semaphore_wait(barrier, SENDERS - 1)


def gather_kernel(k_ref, v_ref, q_ref, do_ref, de_ref, k_all, v_all, q_out, do_out, de_out, kv_send, kv_recv, row_send, row_recv, own_sem):
    me = lax.axis_index("ctx")
    y, x = me // SIDE, me % SIDE
    greet(me)

    def block(ref, i):
        return ref.at[pl.ds(pl.multiple_of(i * BLOCK, BLOCK), BLOCK)]

    def kv_copy(which, src, owner, to, slot):
        whole = (k_all, v_all)[which]
        return pltpu.make_async_remote_copy(
            src_ref=src, dst_ref=block(whole, owner), send_sem=kv_send.at[which, slot], recv_sem=kv_recv.at[which, owner],
            device_id={"ctx": to}, device_id_type=MESH)

    x_peers = [y * SIDE + (x + s) % SIDE for s in (1, 3, 2)]
    y_peers = [((y + s) % SIDE) * SIDE + x for s in (1, 3, 2)]
    own = [pltpu.make_async_copy(k_ref, block(k_all, me), own_sem.at[0]), pltpu.make_async_copy(v_ref, block(v_all, me), own_sem.at[1])]
    sends = []
    for which, ref in ((0, k_ref), (1, v_ref)):
        first, second = ((x_peers, y_peers), (y_peers, x_peers))[which]
        for n, to in enumerate(first + second):
            sends.append(kv_copy(which, ref, me, to, n))
    for c in sends:
        c.start()
    for c in own:
        c.start()

    rows = ((q_ref, q_out), (do_ref, do_out), (de_ref, de_out))

    def row_copy(n, c, r, to):
        src, dst = rows[n]
        return pltpu.make_async_remote_copy(
            src_ref=src.at[c], dst_ref=dst.at[r], send_sem=row_send.at[n, c], recv_sem=row_recv.at[n, r],
            device_id={"ctx": to}, device_id_type=MESH)

    def own_row(n, c, r):
        src, dst = rows[n]
        return pltpu.make_async_copy(src.at[c], dst.at[r], own_sem.at[2 + n])

    for c in range(CHUNKS):
        to = taker_of(me, c)

        @pl.when(to != me)
        def _():
            for n in range(3):
                row_copy(n, c, me // 2, to).start()

        @pl.when(to == me)
        def _():
            for n in range(3):
                own_row(n, c, me // 2).start()

    def arrived(which, owner):
        kv_copy(which, block((k_all, v_all)[which], owner), owner, me, 0).wait_recv()

    for n in range(3):
        for which in (0, 1):
            first, second = ((x_peers, y_peers), (y_peers, x_peers))[which]
            owner = first[n]
            arrived(which, owner)
            for m, to in enumerate(second):
                c = kv_copy(which, block((k_all, v_all)[which], owner), owner, to, 6 + 3 * n + m)
                c.start()
                sends.append(c)
    for which in (0, 1):
        for s in range(1, SIDE):
            for r in range(SIDE):
                if which == 0:
                    arrived(which, ((y + s) % SIDE) * SIDE + (x + r) % SIDE)
                else:
                    arrived(which, ((y + r) % SIDE) * SIDE + (x + s) % SIDE)
    for r in range(CHUNKS):
        source, chunk = source_of(me, r)

        @pl.when(source != me)
        def _():
            for n in range(3):
                row_copy(n, 0, r, me).wait_recv()

        @pl.when(source == me)
        def _():
            for n in range(3):
                own_row(n, chunk, r).wait()

    for c in range(CHUNKS):
        @pl.when(taker_of(me, c) != me)
        def _():
            for n in range(3):
                row_copy(n, c, 0, me).wait_send()

    for c in sends:
        c.wait_send()
    for c in own:
        c.wait()


def gather(k, v, q, do, de):
    anyspace = pl.BlockSpec(memory_space=pl.ANY)
    T = k.shape[0] * SENDERS
    sds = jax.ShapeDtypeStruct
    dma = pltpu.SemaphoreType.DMA
    return pl.pallas_call(
        gather_kernel,
        out_shape=(sds((T, HD), k.dtype), sds((T, HD), k.dtype), sds(q.shape, q.dtype), sds(do.shape, do.dtype), sds(de.shape, de.dtype)),
        in_specs=[anyspace] * 5, out_specs=(anyspace,) * 5,
        scratch_shapes=[dma((2, 15)), dma((2, SENDERS)), dma((3, CHUNKS)), dma((3, CHUNKS)), dma((5,))],
        compiler_params=pltpu.CompilerParams(collective_id=0, has_side_effects=True),
    )(k, v, q, do, de)


def reduce_kernel(dk_ref, dv_ref, dq_ref, dk_out, dv_out, dq_out, own, got, mid, mid_got, send1, recv1, send2, recv2, row_send, row_recv, own_sem):
    me = lax.axis_index("ctx")
    y, x = me // SIDE, me % SIDE
    greet(me)
    steps = (1, 3, 2)

    def lane_of(which):
        return (y, x) if which == 0 else (x, y)

    def peer(which, leg, s):
        along_y = (which == 0) == (leg == 0)
        return ((y + s) % SIDE) * SIDE + x if along_y else y * SIDE + (x + s) % SIDE

    def part(ref, which, at):
        return ref.at[at] if which == 0 else ref.at[:, at]

    copies, local = [], []
    for n, s in enumerate(steps):
        for which, ref in ((0, dk_ref), (1, dv_ref)):
            at = (lane_of(which)[0] + s) % SIDE
            copies.append(pltpu.make_async_remote_copy(
                src_ref=part(ref, which, at), dst_ref=got.at[which, n], send_sem=send1.at[which, n], recv_sem=recv1.at[which, n],
                device_id={"ctx": peer(which, 0, s)}, device_id_type=MESH))
            copies[-1].start()
    for which, ref in ((0, dk_ref), (1, dv_ref)):
        local.append(pltpu.make_async_copy(part(ref, which, lane_of(which)[0]), own.at[which], own_sem.at[which]))
        local[-1].start()

    def row_copy(r, c, to):
        return pltpu.make_async_remote_copy(
            src_ref=dq_ref.at[r], dst_ref=dq_out.at[c], send_sem=row_send.at[r], recv_sem=row_recv.at[c],
            device_id={"ctx": to}, device_id_type=MESH)

    def own_row(r, c):
        return pltpu.make_async_copy(dq_ref.at[r], dq_out.at[c], own_sem.at[2])

    for r in range(CHUNKS):
        to, c = source_of(me, r)

        @pl.when(to != me)
        def _():
            row_copy(r, c, to).start()

        @pl.when(to == me)
        def _():
            own_row(r, c).start()

    late = []
    for which in (0, 1):
        local[which].wait()
        for n in range(3):
            pltpu.make_async_remote_copy(
                src_ref=own.at[which], dst_ref=got.at[which, n], send_sem=send1.at[which, n], recv_sem=recv1.at[which, n],
                device_id={"ctx": me}, device_id_type=MESH).wait_recv()

        def add(i, _, which=which):
            r = pl.ds(pl.multiple_of(i * 128, 128), 128)
            for b in range(SIDE):
                total = own[which, b, r, :].astype(jnp.float32)
                for n in range(3):
                    total = total + got[which, n, b, r, :].astype(jnp.float32)
                mid[which, b, r, :] = total.astype(jnp.bfloat16)
            return 0
        lax.fori_loop(0, BLOCK // 128, add, 0)
        for n, s in enumerate(steps):
            at = (lane_of(which)[1] + s) % SIDE
            late.append(pltpu.make_async_remote_copy(
                src_ref=mid.at[which, at], dst_ref=mid_got.at[which, n], send_sem=send2.at[which, n], recv_sem=recv2.at[which, n],
                device_id={"ctx": peer(which, 1, s)}, device_id_type=MESH))
            late[-1].start()
    for which, ref in ((0, dk_out), (1, dv_out)):
        for n in range(3):
            pltpu.make_async_remote_copy(
                src_ref=mid.at[which, 0], dst_ref=mid_got.at[which, n], send_sem=send2.at[which, n], recv_sem=recv2.at[which, n],
                device_id={"ctx": me}, device_id_type=MESH).wait_recv()

        def last(i, _, which=which, ref=ref):
            r = pl.ds(pl.multiple_of(i * 128, 128), 128)
            total = mid[which, lane_of(which)[1], r, :].astype(jnp.float32)
            for n in range(3):
                total = total + mid_got[which, n, r, :].astype(jnp.float32)
            ref[r, :] = total.astype(jnp.bfloat16)
            return 0
        lax.fori_loop(0, BLOCK // 128, last, 0)
    for c in range(CHUNKS):
        @pl.when(taker_of(me, c) != me)
        def _():
            row_copy(0, c, me).wait_recv()

        @pl.when(taker_of(me, c) == me)
        def _():
            own_row(me // 2, c).wait()

    for r in range(CHUNKS):
        @pl.when(source_of(me, r)[0] != me)
        def _():
            row_copy(r, 0, me).wait_send()

    for c in copies + late:
        c.wait_send()


def reduce(dk, dv, dq):
    anyspace = pl.BlockSpec(memory_space=pl.ANY)
    vm = pl.BlockSpec(memory_space=pltpu.VMEM)
    sds = jax.ShapeDtypeStruct
    dma = pltpu.SemaphoreType.DMA
    bf = jnp.bfloat16
    shape = (SIDE, SIDE, BLOCK, HD)
    return pl.pallas_call(
        reduce_kernel,
        out_shape=(sds((BLOCK, HD), bf), sds((BLOCK, HD), bf), sds(dq.shape, bf)),
        in_specs=[anyspace] * 3, out_specs=(vm, vm, anyspace),
        scratch_shapes=[pltpu.VMEM((2, SIDE, BLOCK, HD), bf), pltpu.VMEM((2, 3, SIDE, BLOCK, HD), bf), pltpu.VMEM((2, SIDE, BLOCK, HD), bf),
            pltpu.VMEM((2, 3, BLOCK, HD), bf), dma((2, 3)), dma((2, 3)), dma((2, 3)), dma((2, 3)), dma((CHUNKS,)), dma((CHUNKS,)), dma((3,))],
        compiler_params=pltpu.CompilerParams(collective_id=1, has_side_effects=True, vmem_limit_bytes=32 * 2**20),
    )(dk.reshape(shape), dv.reshape(shape), dq)


def on_device(queries, attn_keys, attn_values, attn_output, output_grad, chain_lens):
    me = lax.axis_index("ctx")
    ends = jnp.cumsum(chain_lens[0]).astype(jnp.int32)
    delta = jnp.einsum(
        "tphd,tphd->thp",
        output_grad[0].reshape(CHUNKS, TP, GQA, HD),
        attn_output[0].reshape(CHUNKS, TP, GQA, HD),
        preferred_element_type=jnp.float32,
    ).reshape(CHUNKS, 1, R)
    k, v, q, do, delta = gather(
        attn_keys[0],
        attn_values[0],
        queries[0].reshape(CHUNKS, TP, -1),
        output_grad[0].reshape(CHUNKS, TP, -1),
        jnp.broadcast_to(delta, (CHUNKS, 8, R)),
    )
    source, chunk = source_of(me, jnp.arange(CHUNKS, dtype=jnp.int32))
    base = source * BLOCK + chunk * TP
    dq, dk, dv = call(base, ends, q, do, delta, k, v)
    dk, dv, dq = reduce(dk, dv, dq)
    return dq.reshape(1, BLOCK, -1), dk[None], dv[None]


def solution(mesh):
    tok = P("grp", "ctx", None)
    return jax.shard_map(
        on_device,
        mesh=mesh,
        in_specs=(tok, tok, tok, tok, tok, P("grp", None)),
        out_specs=(tok, tok, tok),
        check_vma=False,
    )
```

```python
import functools, math
import jax, jax.numpy as jnp
from jax import lax
from jax.experimental import pallas as pl
from jax.experimental.pallas import tpu as pltpu
from jax.sharding import PartitionSpec as P

HD = 128
GQA = 8
BLOCK = 512
TP = 64
R = TP * GQA
SUB = 128
SB = 64
BIG = 1024
SCALE = HD ** -0.5
C2 = SCALE * math.log2(math.e)
NN = (((1,), (0,)), ((), ()))


def dot(a, b):
    return lax.dot_general(a, b, NN, preferred_element_type=jnp.float32)


def kernel(base_ref, ends_ref, q_ref, do_ref, delta_ref, k_ref, v_ref, dq_ref, dk_ref, dv_ref,
           kt, pbuf, mbuf, mrun, lrun, dka, dva, qs, dos, dqt, qst, dost):
    T = k_ref.shape[0]

    def init(i, _):
        rows = pl.ds(pl.multiple_of(i * 512, 512), 512)
        kt[:, rows] = k_ref[rows, :].T
        dka[rows, :] = jnp.zeros((512, HD), jnp.float32)
        dva[rows, :] = jnp.zeros((512, HD), jnp.float32)
        return 0
    lax.fori_loop(0, T // 512, init, 0)
    e0 = ends_ref[0]
    e1 = ends_ref[1]

    def start_of(p):
        return jnp.where(p < e0, 0, jnp.where(p < e1, e0, e1))

    def tile(t, _):
        p0 = base_ref[t]
        lo = (start_of(p0) // SUB) * SUB
        hi = ((p0 + TP + SUB - 1) // SUB) * SUB
        nb = (hi - lo) // BIG
        rest = (hi - lo) - nb * BIG
        for h in range(GQA):
            qs[h * TP:(h + 1) * TP, :] = q_ref[t, :, h * HD:(h + 1) * HD]
            dos[h * TP:(h + 1) * TP, :] = do_ref[t, :, h * HD:(h + 1) * HD]
        qst[...] = qs[...].T
        dost[...] = dos[...].T
        rpos = p0 + lax.broadcasted_iota(jnp.int32, (1, R), 1) % TP
        rstart = start_of(rpos)
        last_start = start_of(p0 + TP - 1)

        def stats(first, size, masked):
            first = pl.multiple_of(first, SUB)
            s = dot(k_ref[pl.ds(first, size), :], qst[...])
            if masked:
                spos = first + lax.broadcasted_iota(jnp.int32, (size, 1), 0)
                s = jnp.where((spos >= rstart) & (spos <= rpos), s, -1e30)
            s = s.reshape(size // SB, SB // 8, 8, R)
            m = jnp.max(s, axis=1)
            p = jnp.exp2((s - m[:, None]) * C2)
            pbuf[pl.ds(first, size), :] = p.reshape(size, R)
            mbuf[pl.ds(first // SB, size // SB)] = m
            old = mrun[...]
            new = jnp.maximum(old, jnp.max(m, axis=0))
            lrun[...] = lrun[...] * jnp.exp2((old - new) * C2) + jnp.sum(jnp.sum(p, axis=1) * jnp.exp2((m - new) * C2), axis=0)
            mrun[...] = new

        def grads(first, size):
            first = pl.multiple_of(first, SUB)
            rows = pl.ds(first, size)
            f = jnp.exp2((mbuf[pl.ds(first // SB, size // SB)] - top) * C2) * linv
            p = (pbuf[rows, :].reshape(size // SB, SB // 8, 8, R) * f[:, None]).reshape(size, R)
            dp = dot(v_ref[rows, :], dost[...])
            ds = (p * (dp - delta)).astype(jnp.bfloat16)
            dva[rows, :] += dot(p.astype(jnp.bfloat16), dos[...])
            dka[rows, :] += dot(ds, qs[...])
            dqt[...] += dot(kt[:, rows], ds)

        def sweep(body):
            def big(j, _):
                body(lo + j * BIG, BIG)
                return 0
            lax.fori_loop(0, nb, big, 0)
            at = lo + nb * BIG
            size = BIG // 2
            while size >= SUB:
                has = (rest & size) != 0
                pl.when(has)(functools.partial(body, at, size))
                at = at + jnp.where(has, size, 0)
                size //= 2

        def stats_any(first, size):
            need = (first < last_start) | (first + size - 1 > p0)
            pl.when(need)(lambda: stats(first, size, True))
            pl.when(jnp.logical_not(need))(lambda: stats(first, size, False))
        mrun[...] = jnp.full((8, R), -1e30, jnp.float32)
        lrun[...] = jnp.zeros((8, R), jnp.float32)
        sweep(stats_any)
        top = jnp.max(mrun[...], axis=0, keepdims=True)
        linv = 1.0 / jnp.sum(lrun[...] * jnp.exp2((mrun[...] - top) * C2), axis=0, keepdims=True)
        delta = delta_ref[t, 0:1, :]
        dqt[...] = jnp.zeros((HD, R), jnp.float32)
        sweep(grads)
        dq = (dqt[...].T * SCALE).astype(jnp.bfloat16)
        for h in range(GQA):
            dq_ref[t, :, h * HD:(h + 1) * HD] = dq[h * TP:(h + 1) * TP, :]
        return 0
    lax.fori_loop(0, q_ref.shape[0], tile, 0)

    def fin(i, _):
        rows = pl.ds(pl.multiple_of(i * 512, 512), 512)
        dk_ref[rows, :] = (dka[rows, :] * SCALE).astype(dk_ref.dtype)
        dv_ref[rows, :] = dva[rows, :].astype(dv_ref.dtype)
        return 0
    lax.fori_loop(0, T // 512, fin, 0)


def call(base, ends, q, do, delta, k, v):
    T = k.shape[0]
    vm = pl.BlockSpec(memory_space=pltpu.VMEM)
    sm = pl.BlockSpec(memory_space=pltpu.SMEM)
    f32 = jnp.float32
    bf = jnp.bfloat16
    return pl.pallas_call(
        kernel,
        out_shape=(jax.ShapeDtypeStruct(q.shape, bf), jax.ShapeDtypeStruct((T, HD), bf), jax.ShapeDtypeStruct((T, HD), bf)),
        in_specs=[sm, sm, vm, vm, vm, vm, vm],
        out_specs=(vm, vm, vm),
        scratch_shapes=[pltpu.VMEM((HD, T), bf), pltpu.VMEM((T, R), f32), pltpu.VMEM((T // SB, 8, R), f32), pltpu.VMEM((8, R), f32), pltpu.VMEM((8, R), f32),
            pltpu.VMEM((T, HD), f32), pltpu.VMEM((T, HD), f32), pltpu.VMEM((R, HD), bf), pltpu.VMEM((R, HD), bf), pltpu.VMEM((HD, R), f32),
            pltpu.VMEM((HD, R), bf), pltpu.VMEM((HD, R), bf)],
        compiler_params=pltpu.CompilerParams(vmem_limit_bytes=60 * 2**20),
    )(base, ends, q, do, delta, k, v)


MESH = pl.DeviceIdType.MESH
SIDE = 4
SENDERS = SIDE * SIDE
CHUNKS = 8


def source_of(dev, r):
    y, x = dev // SIDE, dev % SIDE
    ahead = (x - 2 * (r % 2) + SIDE) % SIDE
    upper = jnp.where((ahead == 1) | (ahead == 2), 1, 0)
    far = jnp.where(ahead >= 2, 1, 0)
    chunk = 2 * jnp.where(r % 2 == 0, y, SIDE - 1 - y) + far
    return 2 * r + upper, chunk


def taker_of(owner, c):
    r, upper, far = owner // 2, owner % 2, c % 2
    x = (2 * (r % 2) + jnp.where(upper == 1, 1 + far, SIDE - far)) % SIDE
    y = jnp.where(r % 2 == 0, c // 2, SIDE - 1 - c // 2)
    return y * SIDE + x


def at(y, x):
    return (y + SIDE) % SIDE * SIDE + (x + SIDE) % SIDE


def greet(me):
    barrier = pltpu.get_barrier_semaphore()
    for step in range(1, SENDERS):
        pl.semaphore_signal(barrier, inc=1, device_id={"ctx": (me + step) % SENDERS}, device_id_type=MESH)
    pl.semaphore_wait(barrier, SENDERS - 1)


def send(src, dst, send_sem, recv_sem, to):
    return pltpu.make_async_remote_copy(
        src_ref=src, dst_ref=dst, send_sem=send_sem, recv_sem=recv_sem, device_id={"ctx": to}, device_id_type=MESH)


def gather_kernel(k_ref, v_ref, q_ref, do_ref, de_ref, k_all, v_all, q_out, do_out, de_out,
                  hold, kv_send, kv_recv, row_send, row_recv, hop_recv, on_send, own_sem):
    me = lax.axis_index("ctx")
    y, x = me // SIDE, me % SIDE
    greet(me)
    HALF = BLOCK // 2

    def block(which, i, half=None):
        first, size = (i * BLOCK, BLOCK) if half is None else (i * BLOCK + half * HALF, HALF)
        return (k_all, v_all)[which].at[pl.ds(pl.multiple_of(first, HALF), size)]

    sent = []

    def push(which, slot, owner, to, half=None, src=None):
        c = send(block(which, owner, half) if src is None else src, block(which, owner, half),
                 kv_send.at[which, slot], kv_recv.at[which, owner, 0 if half is None else half], to)
        c.start()
        sent.append(c)

    def arrived(which, owner, half=None):
        b = block(which, owner, half)
        send(b, b, kv_send.at[which, 0], kv_recv.at[which, owner, 0 if half is None else half], me).wait_recv()

    def place(which, first, second):
        return at(y + second, x + first) if which == 0 else at(y + first, x + second)

    own = [pltpu.make_async_copy(ref, block(w, me), own_sem.at[w]) for w, ref in ((0, k_ref), (1, v_ref))]
    for w, ref in ((0, k_ref), (1, v_ref)):
        push(w, 0, me, place(w, 1, 0), src=ref)
        push(w, 1, me, place(w, -1, 0), src=ref)
    for w, ref in ((0, k_ref), (1, v_ref)):
        push(w, 4, me, place(w, 0, 1), src=ref)
        push(w, 5, me, place(w, 0, -1), src=ref)
    for c in own:
        c.start()

    rows = ((q_ref, q_out), (do_ref, do_out), (de_ref, de_out))

    def row_copy(n, c, r, to):
        src, dst = rows[n]
        return send(src.at[c], dst.at[r], row_send.at[n, c], row_recv.at[n, r], to)

    def hop_copy(n, c, side, to):
        return send(rows[n][0].at[c], hold.at[n, side], row_send.at[n, c], hop_recv.at[n, side], to)

    def on_copy(n, side, r, to):
        return send(hold.at[n, side], rows[n][1].at[r], on_send.at[n, side], row_recv.at[n, r], to)

    def own_row(n, c, r):
        src, dst = rows[n]
        return pltpu.make_async_copy(src.at[c], dst.at[r], own_sem.at[2 + n])

    def send_rows():
        for c in list(range(0, CHUNKS)):
            to = taker_of(me, c)
            opposite = to // SIDE == (y + 2) % SIDE
            side = c % 2

            @pl.when(opposite)
            def _():
                hop = at(y + 1, x) if side == 0 else at(y - 1, to % SIDE)
                for n in range(2):
                    hop_copy(n, c, side, hop).start()
                row_copy(2, c, me // 2, to).start()

            @pl.when(jnp.logical_not(opposite) & (to != me))
            def _():
                for n in range(3):
                    row_copy(n, c, me // 2, to).start()

            @pl.when(to == me)
            def _():
                for n in range(3):
                    own_row(n, c, me // 2).start()

    def pass_on():
        for side in range(2):
            owner = at(y - 1, x) if side == 0 else at(y + 1, jnp.where(x % 2 == 1, x + 1, x - 1))
            to = at(y + 1, x) if side == 0 else at(y - 1, x)
            for n in range(2):
                hop_copy(n, 0, side, me).wait_recv()
                on_copy(n, side, owner // 2, to).start()

    send_rows()
    for w in (0, 1):
        b = place(w, -1, 0)
        arrived(w, b)
        push(w, 2, b, place(w, 1, 0), half=0)
        b = place(w, 1, 0)
        arrived(w, b)
        push(w, 3, b, place(w, -1, 0), half=1)
    for n, s in ((1, 1), (2, -1)):
        for w in (0, 1):
            b = place(w, s, 0)
            push(w, 4 + 4 * n, b, place(w, 0, 1))
            push(w, 5 + 4 * n, b, place(w, 0, -1))
    for w in (0, 1):
        b = place(w, 2, 0)
        arrived(w, b, 0)
        arrived(w, b, 1)
        push(w, 16, b, place(w, 0, 1))
        push(w, 17, b, place(w, 0, -1))
    pass_on()
    for n, s in ((0, 0), (1, 1), (2, -1), (3, 2)):
        for w in (0, 1):
            b = place(w, s, -1)
            arrived(w, b)
            push(w, 6 + 4 * n, b, place(w, 0, 1), half=0)
            b = place(w, s, 1)
            arrived(w, b)
            push(w, 7 + 4 * n, b, place(w, 0, -1), half=1)
    for n, s in ((0, 0), (1, 1), (2, -1), (3, 2)):
        for w in (0, 1):
            b = place(w, s, 2)
            arrived(w, b, 0)
            arrived(w, b, 1)

    for r in range(CHUNKS):
        source, chunk = source_of(me, r)

        @pl.when(source != me)
        def _():
            for n in range(3):
                row_copy(n, 0, r, me).wait_recv()

        @pl.when(source == me)
        def _():
            for n in range(3):
                own_row(n, chunk, r).wait()

    for c in range(CHUNKS):
        @pl.when(taker_of(me, c) != me)
        def _():
            for n in range(3):
                row_copy(n, c, 0, me).wait_send()

    for side in range(2):
        for n in range(2):
            on_copy(n, side, 0, me).wait_send()
    for c in sent:
        c.wait_send()
    for c in own:
        c.wait()


def gather(k, v, q, do, de):
    anyspace = pl.BlockSpec(memory_space=pl.ANY)
    T = k.shape[0] * SENDERS
    sds = jax.ShapeDtypeStruct
    dma = pltpu.SemaphoreType.DMA
    return pl.pallas_call(
        gather_kernel,
        out_shape=(sds((T, HD), k.dtype), sds((T, HD), k.dtype), sds(q.shape, q.dtype), sds(do.shape, do.dtype), sds(de.shape, de.dtype)),
        in_specs=[anyspace] * 5, out_specs=(anyspace,) * 5,
        scratch_shapes=[pltpu.VMEM((2, 2) + q.shape[1:], q.dtype), dma((2, 20)), dma((2, SENDERS, 2)), dma((3, CHUNKS)), dma((3, CHUNKS)),
            dma((2, 2)), dma((2, 2)), dma((5,))],
        compiler_params=pltpu.CompilerParams(collective_id=0, has_side_effects=True),
    )(k, v, q, do, de)


def reduce_kernel(dk_ref, dv_ref, dq_ref, dk_out, dv_out, dq_out, via, got, mid, via2, got2, hold,
                  send1, recv1, send2, recv2, row_send, row_recv, hop_recv, on_send, own_sem):
    me = lax.axis_index("ctx")
    y, x = me // SIDE, me % SIDE
    greet(me)
    HALF = BLOCK // 2
    refs = (dk_ref, dv_ref)
    outs = (dk_out, dv_out)
    sent = []

    def lane(w, leg):
        return (y, x)[(w + leg) % 2]

    def peer(w, leg, s):
        return at(y + s, x) if (w + leg) % 2 == 0 else at(y, x + s)

    def part(w, s, half):
        line = (lane(w, 0) + s + SIDE) % SIDE
        two = pl.ds(2 * half, 2)
        return refs[w].at[line, two] if w == 0 else refs[w].at[two, line]

    def push(src, dst, ssem, rsem, to):
        c = send(src, dst, ssem, rsem, to)
        c.start()
        sent.append(c)

    for w in (0, 1):
        up, down = peer(w, 0, 1), peer(w, 0, -1)
        push(part(w, 2, 0), via.at[w, 0], send1.at[w, 0], recv1.at[w, 0], up)
        push(part(w, 2, 1), via.at[w, 1], send1.at[w, 1], recv1.at[w, 1], down)
    for w in (0, 1):
        up, down = peer(w, 0, 1), peer(w, 0, -1)
        push(part(w, 1, 1), got.at[w, 0, 1], send1.at[w, 3], recv1.at[w, 3], up)
        push(part(w, -1, 0), got.at[w, 1, 0], send1.at[w, 4], recv1.at[w, 4], down)

    def row_copy(r, c, to):
        return send(dq_ref.at[r], dq_out.at[c], row_send.at[r], row_recv.at[c], to)

    def hop_copy(r, side, to):
        return send(dq_ref.at[r], hold.at[side], row_send.at[r], hop_recv.at[side], to)

    def on_copy(side, c, to):
        return send(hold.at[side], dq_out.at[c], on_send.at[side], row_recv.at[c], to)

    def own_row(r, c):
        return pltpu.make_async_copy(dq_ref.at[r], dq_out.at[c], own_sem.at[0])

    for r in range(CHUNKS):
        to, c = source_of(me, r)
        opposite = r // 2 == (y + 2) % SIDE
        far = c % 2

        @pl.when(opposite & (far == 0))
        def _():
            hop_copy(r, 0, at(y + 1, x)).start()

        @pl.when(opposite & (far == 1))
        def _():
            hop_copy(r, 1, at(y - 1, to % SIDE)).start()

        @pl.when(jnp.logical_not(opposite) & (to != me))
        def _():
            row_copy(r, c, to).start()

        @pl.when(to == me)
        def _():
            own_row(r, c).start()

    def wait1(w, slot, dst):
        send(dst, dst, send1.at[w, slot], recv1.at[w, slot], me).wait_recv()

    def tile(i):
        return pl.ds(pl.multiple_of(i * 128, 128), 128)

    for w in (0, 1):
        for d in (0, 1):
            wait1(w, d, via.at[w, d])
            line = (lane(w, 0) + (1 if d == 0 else 3)) % SIDE

            def add(i, _, w=w, d=d, line=line):
                r = tile(i)
                for b in range(2):
                    mine = refs[w][line, 2 * d + b, r, :] if w == 0 else refs[w][2 * d + b, line, r, :]
                    via[w, d, b, r, :] = (via[w, d, b, r, :].astype(jnp.float32) + mine.astype(jnp.float32)).astype(jnp.bfloat16)
                return 0
            lax.fori_loop(0, BLOCK // 128, add, 0)
            push(via.at[w, d], got.at[w, d, d], send1.at[w, 2 if d == 0 else 5], recv1.at[w, 2 if d == 0 else 5],
                 peer(w, 0, 1 if d == 0 else -1))

    for side in range(2):
        owner = at(y + 1, x) if side == 0 else at(y - 1, x)
        taker = at(y - 1, x) if side == 0 else at(y + 1, jnp.where(x % 2 == 0, x - 1, x + 1))
        reverse = (owner // 2) % 2 == 1
        c = 2 * jnp.where(reverse, SIDE - 1 - taker // SIDE, taker // SIDE) + side
        hop_copy(0, side, me).wait_recv()
        on_copy(side, c, owner).start()

    for w in (0, 1):
        for slot, d, h in ((3, 0, 1), (4, 1, 0), (2, 0, 0), (5, 1, 1)):
            wait1(w, slot, got.at[w, d, h])
        line = lane(w, 0)

        def add4(i, _, w=w, line=line):
            r = tile(i)
            for b in range(SIDE):
                mine = refs[w][line, b, r, :] if w == 0 else refs[w][b, line, r, :]
                total = mine.astype(jnp.float32) + got[w, 0, b // 2, b % 2, r, :].astype(jnp.float32)
                mid[w, b, r, :] = (total + got[w, 1, b // 2, b % 2, r, :].astype(jnp.float32)).astype(jnp.bfloat16)
            return 0
        lax.fori_loop(0, BLOCK // 128, add4, 0)

        def half2(s, h, w=w):
            return mid.at[w, (lane(w, 1) + s + SIDE) % SIDE, pl.ds(h * HALF, HALF)]
        up, down = peer(w, 1, 1), peer(w, 1, -1)
        push(half2(2, 0), via2.at[w, 0], send2.at[w, 0], recv2.at[w, 0], up)
        push(half2(2, 1), via2.at[w, 1], send2.at[w, 1], recv2.at[w, 1], down)
        push(half2(1, 1), got2.at[w, 0, 1], send2.at[w, 3], recv2.at[w, 3], up)
        push(half2(-1, 0), got2.at[w, 1, 0], send2.at[w, 4], recv2.at[w, 4], down)

    def wait2(w, slot, dst):
        send(dst, dst, send2.at[w, slot], recv2.at[w, slot], me).wait_recv()

    for w in (0, 1):
        for d in (0, 1):
            wait2(w, d, via2.at[w, d])
            line = (lane(w, 1) + (1 if d == 0 else 3)) % SIDE
            for i in range(2):
                r = pl.ds(i * 128, 128)
                mine = mid[w, line, pl.ds(d * HALF + i * 128, 128), :]
                via2[w, d, r, :] = (via2[w, d, r, :].astype(jnp.float32) + mine.astype(jnp.float32)).astype(jnp.bfloat16)
            push(via2.at[w, d], got2.at[w, d, d], send2.at[w, 2 if d == 0 else 5], recv2.at[w, 2 if d == 0 else 5],
                 peer(w, 1, 1 if d == 0 else -1))
    for w in (0, 1):
        for slot, d, h in ((3, 0, 1), (4, 1, 0), (2, 0, 0), (5, 1, 1)):
            wait2(w, slot, got2.at[w, d, h])
        for h in (0, 1):
            for i in range(2):
                r = pl.ds(i * 128, 128)
                out = pl.ds(h * HALF + i * 128, 128)
                total = mid[w, lane(w, 1), out, :].astype(jnp.float32) + got2[w, 0, h, r, :].astype(jnp.float32)
                outs[w][out, :] = (total + got2[w, 1, h, r, :].astype(jnp.float32)).astype(jnp.bfloat16)
    for c in range(CHUNKS):
        @pl.when(taker_of(me, c) != me)
        def _():
            row_copy(0, c, me).wait_recv()

        @pl.when(taker_of(me, c) == me)
        def _():
            own_row(me // 2, c).wait()

    for r in range(CHUNKS):
        @pl.when(source_of(me, r)[0] != me)
        def _():
            row_copy(r, 0, me).wait_send()

    for side in range(2):
        on_copy(side, 0, me).wait_send()
    for c in sent:
        c.wait_send()


def reduce(dk, dv, dq):
    anyspace = pl.BlockSpec(memory_space=pl.ANY)
    vm = pl.BlockSpec(memory_space=pltpu.VMEM)
    sds = jax.ShapeDtypeStruct
    dma = pltpu.SemaphoreType.DMA
    bf = jnp.bfloat16
    half = BLOCK // 2
    shape = (SIDE, SIDE, BLOCK, HD)
    return pl.pallas_call(
        reduce_kernel,
        out_shape=(sds((BLOCK, HD), bf), sds((BLOCK, HD), bf), sds(dq.shape, bf)),
        in_specs=[vm, vm, anyspace], out_specs=(vm, vm, anyspace),
        scratch_shapes=[pltpu.VMEM((2, 2, 2, BLOCK, HD), bf), pltpu.VMEM((2, 2, 2, 2, BLOCK, HD), bf), pltpu.VMEM((2, SIDE, BLOCK, HD), bf),
            pltpu.VMEM((2, 2, half, HD), bf), pltpu.VMEM((2, 2, 2, half, HD), bf), pltpu.VMEM((2,) + dq.shape[1:], bf),
            dma((2, 6)), dma((2, 6)), dma((2, 6)), dma((2, 6)), dma((CHUNKS,)), dma((CHUNKS,)), dma((2,)), dma((2,)), dma((1,))],
        compiler_params=pltpu.CompilerParams(collective_id=1, has_side_effects=True, vmem_limit_bytes=32 * 2**20),
    )(dk.reshape(shape), dv.reshape(shape), dq)


def on_device(queries, attn_keys, attn_values, attn_output, output_grad, chain_lens):
    me = lax.axis_index("ctx")
    ends = jnp.cumsum(chain_lens[0]).astype(jnp.int32)
    delta = jnp.einsum(
        "tphd,tphd->thp",
        output_grad[0].reshape(CHUNKS, TP, GQA, HD),
        attn_output[0].reshape(CHUNKS, TP, GQA, HD),
        preferred_element_type=jnp.float32,
    ).reshape(CHUNKS, 1, R)
    k, v, q, do, delta = gather(
        attn_keys[0],
        attn_values[0],
        queries[0].reshape(CHUNKS, TP, -1),
        output_grad[0].reshape(CHUNKS, TP, -1),
        jnp.broadcast_to(delta, (CHUNKS, 8, R)),
    )
    source, chunk = source_of(me, jnp.arange(CHUNKS, dtype=jnp.int32))
    base = source * BLOCK + chunk * TP
    dq, dk, dv = call(base, ends, q, do, delta, k, v)
    dk, dv, dq = reduce(dk, dv, dq)
    return dq.reshape(1, BLOCK, -1), dk[None], dv[None]


def solution(mesh):
    tok = P("grp", "ctx", None)
    return jax.shard_map(
        on_device,
        mesh=mesh,
        in_specs=(tok, tok, tok, tok, tok, P("grp", None)),
        out_specs=(tok, tok, tok),
        check_vma=False,
    )
```

```python
import functools, math
import jax, jax.numpy as jnp
from jax import lax
from jax.experimental import pallas as pl
from jax.experimental.pallas import tpu as pltpu
from jax.sharding import PartitionSpec as P

HD = 128
GQA = 8
BLOCK = 512
TP = 64
R = TP * GQA
SUB = 128
SB = 64
BIG = 1024
SCALE = HD ** -0.5
STEP = 256
C2 = SCALE * math.log2(math.e)
NN = (((1,), (0,)), ((), ()))


def dot(a, b):
    return lax.dot_general(a, b, NN, preferred_element_type=jnp.float32)


def kernel(base_ref, ends_ref, q_ref, do_ref, delta_ref, k_ref, v_any, dq_any, dk_any, dv_any,
           kt, pbuf, mbuf, mrun, lrun, dka, dva, qs, dos, dqt, qst, dost, v_ref, dq_ref, dk_ref, dv_ref, sem, out_sem):
    T = k_ref.shape[0]

    fetch_v = pltpu.make_async_copy(v_any, v_ref, sem.at[0])
    fetch_v.start()

    def init(i, _):
        rows = pl.ds(pl.multiple_of(i * 512, 512), 512)
        kt[:, rows] = k_ref[rows, :].T
        dka[rows, :] = jnp.zeros((512, HD), jnp.float32)
        dva[rows, :] = jnp.zeros((512, HD), jnp.float32)
        return 0
    lax.fori_loop(0, T // 512, init, 0)
    fetch_v.wait()
    e0 = ends_ref[0]
    e1 = ends_ref[1]

    def dq_out(t):
        return pltpu.make_async_copy(dq_ref.at[t], dq_any.at[t], sem.at[1 + t])

    def start_of(p):
        return jnp.where(p < e0, 0, jnp.where(p < e1, e0, e1))

    def tile(t, _):
        p0 = base_ref[t]
        lo = (start_of(p0) // SUB) * SUB
        hi = ((p0 + TP + SUB - 1) // SUB) * SUB
        odd = (hi - lo) % STEP != 0
        hi = jnp.where(odd & (lo == 0), hi + SUB, hi)
        lo = jnp.where(odd & (lo > 0), lo - SUB, lo)
        nb = (hi - lo) // BIG
        rest = (hi - lo) - nb * BIG
        for h in range(GQA):
            qs[h * TP:(h + 1) * TP, :] = q_ref[t, :, h * HD:(h + 1) * HD]
            dos[h * TP:(h + 1) * TP, :] = do_ref[t, :, h * HD:(h + 1) * HD]
        qst[...] = qs[...].T
        dost[...] = dos[...].T
        rpos = p0 + lax.broadcasted_iota(jnp.int32, (1, R), 1) % TP
        rstart = start_of(rpos)
        last_start = start_of(p0 + TP - 1)

        def stats(first, size, masked):
            first = pl.multiple_of(first, SUB)
            s = dot(k_ref[pl.ds(first, size), :], qst[...])
            if masked:
                spos = first + lax.broadcasted_iota(jnp.int32, (size, 1), 0)
                s = jnp.where((spos >= rstart) & (spos <= rpos), s, -1e30)
            s = s.reshape(size // SB, SB // 8, 8, R)
            m = jnp.max(s, axis=1)
            p = jnp.exp2((s - m[:, None]) * C2)
            pbuf[pl.ds(first, size), :] = p.reshape(size, R)
            mbuf[pl.ds(first // SB, size // SB)] = m
            old = mrun[...]
            new = jnp.maximum(old, jnp.max(m, axis=0))
            lrun[...] = lrun[...] * jnp.exp2((old - new) * C2) + jnp.sum(jnp.sum(p, axis=1) * jnp.exp2((m - new) * C2), axis=0)
            mrun[...] = new

        def grads(first, size):
            first = pl.multiple_of(first, SUB)
            rows = pl.ds(first, size)
            f = jnp.exp2((mbuf[pl.ds(first // SB, size // SB)] - top) * C2) * linv
            p = (pbuf[rows, :].reshape(size // SB, SB // 8, 8, R) * f[:, None]).reshape(size, R)
            dp = dot(v_ref[rows, :], dost[...])
            ds = (p * (dp - delta)).astype(jnp.bfloat16)
            dva[rows, :] += dot(p.astype(jnp.bfloat16), dos[...])
            dka[rows, :] += dot(ds, qs[...])
            dqt[...] += dot(kt[:, rows], ds)

        def sweep(body, last):
            def big(j, _):
                body(lo + j * BIG, BIG)
                return 0
            lax.fori_loop(0, nb, big, 0)
            at = lo + nb * BIG
            for size in range(STEP, BIG, STEP):
                pl.when(rest == size)(functools.partial(last, at, size))

        def stats_any(first, size):
            need = (first < last_start) | (first + size - 1 > p0)
            pl.when(need)(lambda: stats(first, size, True))
            pl.when(jnp.logical_not(need))(lambda: stats(first, size, False))
        mrun[...] = jnp.full((8, R), -1e30, jnp.float32)
        lrun[...] = jnp.zeros((8, R), jnp.float32)
        sweep(stats_any, functools.partial(stats, masked=True))
        top = jnp.max(mrun[...], axis=0, keepdims=True)
        linv = 1.0 / jnp.sum(lrun[...] * jnp.exp2((mrun[...] - top) * C2), axis=0, keepdims=True)
        delta = delta_ref[t, 0:1, :]
        dqt[...] = jnp.zeros((HD, R), jnp.float32)
        sweep(grads, grads)
        dq = (dqt[...].T * SCALE).astype(jnp.bfloat16)
        for h in range(GQA):
            dq_ref[t, :, h * HD:(h + 1) * HD] = dq[h * TP:(h + 1) * TP, :]
        dq_out(t).start()
        return 0
    lax.fori_loop(0, q_ref.shape[0], tile, 0)

    def part_out(i, n):
        rows = pl.ds(pl.multiple_of(i * 1024, 1024), 1024)
        src, dst = ((dk_ref, dk_any), (dv_ref, dv_any))[n]
        return pltpu.make_async_copy(src.at[rows], dst.at[rows], out_sem.at[n, i])

    def fin(i, _):
        rows = pl.ds(pl.multiple_of(i * 1024, 1024), 1024)
        dk_ref[rows, :] = (dka[rows, :] * SCALE).astype(dk_ref.dtype)
        dv_ref[rows, :] = dva[rows, :].astype(dv_ref.dtype)
        part_out(i, 0).start()
        part_out(i, 1).start()
        return 0
    lax.fori_loop(0, T // 1024, fin, 0)

    def drain(i, _):
        part_out(i, 0).wait()
        part_out(i, 1).wait()
        return 0
    lax.fori_loop(0, T // 1024, drain, 0)

    def drain_q(t, _):
        dq_out(t).wait()
        return 0
    lax.fori_loop(0, q_ref.shape[0], drain_q, 0)


def call(base, ends, q, do, delta, k, v):
    T = k.shape[0]
    vm = pl.BlockSpec(memory_space=pltpu.VMEM)
    sm = pl.BlockSpec(memory_space=pltpu.SMEM)
    hbm = pl.BlockSpec(memory_space=pl.ANY)
    f32 = jnp.float32
    bf = jnp.bfloat16
    return pl.pallas_call(
        kernel,
        out_shape=(jax.ShapeDtypeStruct(q.shape, bf), jax.ShapeDtypeStruct((T, HD), bf), jax.ShapeDtypeStruct((T, HD), bf)),
        in_specs=[sm, sm, vm, vm, vm, vm, hbm],
        out_specs=(hbm, hbm, hbm),
        scratch_shapes=[pltpu.VMEM((HD, T), bf), pltpu.VMEM((T, R), f32), pltpu.VMEM((T // SB, 8, R), f32), pltpu.VMEM((8, R), f32), pltpu.VMEM((8, R), f32),
            pltpu.VMEM((T, HD), f32), pltpu.VMEM((T, HD), f32), pltpu.VMEM((R, HD), bf), pltpu.VMEM((R, HD), bf), pltpu.VMEM((HD, R), f32),
            pltpu.VMEM((HD, R), bf), pltpu.VMEM((HD, R), bf),
            pltpu.VMEM((T, HD), bf), pltpu.VMEM(q.shape, bf), pltpu.VMEM((T, HD), bf), pltpu.VMEM((T, HD), bf),
            pltpu.SemaphoreType.DMA((1 + q.shape[0],)), pltpu.SemaphoreType.DMA((2, T // 1024))],
        compiler_params=pltpu.CompilerParams(vmem_limit_bytes=60 * 2**20),
    )(base, ends, q, do, delta, k, v)


MESH = pl.DeviceIdType.MESH
SIDE = 4
SENDERS = SIDE * SIDE
CHUNKS = 8


def source_of(dev, r):
    y, x = dev // SIDE, dev % SIDE
    ahead = (x - 2 * (r % 2) + SIDE) % SIDE
    upper = jnp.where((ahead == 1) | (ahead == 2), 1, 0)
    far = jnp.where(ahead >= 2, 1, 0)
    chunk = 2 * jnp.where(r % 2 == 0, y, SIDE - 1 - y) + far
    return 2 * r + upper, chunk


def taker_of(owner, c):
    r, upper, far = owner // 2, owner % 2, c % 2
    x = (2 * (r % 2) + jnp.where(upper == 1, 1 + far, SIDE - far)) % SIDE
    y = jnp.where(r % 2 == 0, c // 2, SIDE - 1 - c // 2)
    return y * SIDE + x


def at(y, x):
    return (y + SIDE) % SIDE * SIDE + (x + SIDE) % SIDE


def greet(me):
    barrier = pltpu.get_barrier_semaphore()
    for step in range(1, SENDERS):
        pl.semaphore_signal(barrier, inc=1, device_id={"ctx": (me + step) % SENDERS}, device_id_type=MESH)
    pl.semaphore_wait(barrier, SENDERS - 1)


def send(src, dst, send_sem, recv_sem, to):
    return pltpu.make_async_remote_copy(
        src_ref=src, dst_ref=dst, send_sem=send_sem, recv_sem=recv_sem, device_id={"ctx": to}, device_id_type=MESH)


def gather_kernel(k_ref, v_ref, q_ref, do_ref, o_ref, k_all, v_all, q_out, do_out, de_out,
                  do_v, o_v, de_ref, hold, kv_send, kv_recv, row_send, row_recv, hop_recv, on_send, own_sem):
    me = lax.axis_index("ctx")
    y, x = me // SIDE, me % SIDE
    fetch = [pltpu.make_async_copy(do_ref, do_v, own_sem.at[5]), pltpu.make_async_copy(o_ref, o_v, own_sem.at[6])]
    for c in fetch:
        c.start()
    greet(me)
    HALF = BLOCK // 2

    def block(which, i, half=None):
        first, size = (i * BLOCK, BLOCK) if half is None else (i * BLOCK + half * HALF, HALF)
        return (k_all, v_all)[which].at[pl.ds(pl.multiple_of(first, HALF), size)]

    sent = []

    def push(which, slot, owner, to, half=None, src=None):
        c = send(block(which, owner, half) if src is None else src, block(which, owner, half),
                 kv_send.at[which, slot], kv_recv.at[which, owner, 0 if half is None else half], to)
        c.start()
        sent.append(c)

    def arrived(which, owner, half=None):
        b = block(which, owner, half)
        send(b, b, kv_send.at[which, 0], kv_recv.at[which, owner, 0 if half is None else half], me).wait_recv()

    def place(which, first, second):
        return at(y + second, x + first) if which == 0 else at(y + first, x + second)

    own = [pltpu.make_async_copy(ref, block(w, me), own_sem.at[w]) for w, ref in ((0, k_ref), (1, v_ref))]
    for w, ref in ((0, k_ref), (1, v_ref)):
        push(w, 0, me, place(w, 1, 0), src=ref)
        push(w, 1, me, place(w, -1, 0), src=ref)
    for w, ref in ((0, k_ref), (1, v_ref)):
        push(w, 4, me, place(w, 0, 1), src=ref)
        push(w, 5, me, place(w, 0, -1), src=ref)
    for c in own:
        c.start()

    rows = ((q_ref, q_out), (do_ref, do_out), (de_ref, de_out))

    def row_copy(n, c, r, to):
        src, dst = rows[n]
        return send(src.at[c], dst.at[r], row_send.at[n, c], row_recv.at[n, r], to)

    def hop_copy(n, c, side, to):
        return send(rows[n][0].at[c], hold.at[n, side], row_send.at[n, c], hop_recv.at[n, side], to)

    def on_copy(n, side, r, to):
        return send(hold.at[n, side], rows[n][1].at[r], on_send.at[n, side], row_recv.at[n, r], to)

    def own_row(n, c, r):
        src, dst = rows[n]
        return pltpu.make_async_copy(src.at[c], dst.at[r], own_sem.at[2 + n])

    def send_rows():
        for c in range(CHUNKS):
            to = taker_of(me, c)
            opposite = to // SIDE == (y + 2) % SIDE
            side = c % 2

            @pl.when(opposite)
            def _():
                hop = at(y + 1, x) if side == 0 else at(y - 1, to % SIDE)
                for n in range(2):
                    hop_copy(n, c, side, hop).start()

            @pl.when(jnp.logical_not(opposite) & (to != me))
            def _():
                for n in range(2):
                    row_copy(n, c, me // 2, to).start()

            @pl.when(to == me)
            def _():
                for n in range(2):
                    own_row(n, c, me // 2).start()

    def send_deltas():
        for c in fetch:
            c.wait()
        ones = jnp.ones((8, HD), jnp.float32)

        def chunk(c, _):
            for h in range(GQA):
                lanes = slice(h * HD, (h + 1) * HD)
                prod = do_v[c, :, lanes].astype(jnp.float32) * o_v[c, :, lanes].astype(jnp.float32)
                de_ref[c, :, h * TP:(h + 1) * TP] = lax.dot_general(
                    ones, prod, (((1,), (1,)), ((), ())), precision=lax.Precision.HIGHEST, preferred_element_type=jnp.float32)
            return 0
        lax.fori_loop(0, CHUNKS, chunk, 0)
        for c in range(CHUNKS):
            to = taker_of(me, c)

            @pl.when(to != me)
            def _():
                row_copy(2, c, me // 2, to).start()

            @pl.when(to == me)
            def _():
                own_row(2, c, me // 2).start()

    def pass_on():
        for side in range(2):
            owner = at(y - 1, x) if side == 0 else at(y + 1, jnp.where(x % 2 == 1, x + 1, x - 1))
            to = at(y + 1, x) if side == 0 else at(y - 1, x)
            for n in range(2):
                hop_copy(n, 0, side, me).wait_recv()
                on_copy(n, side, owner // 2, to).start()

    send_rows()
    send_deltas()
    for w in (0, 1):
        b = place(w, -1, 0)
        arrived(w, b)
        push(w, 2, b, place(w, 1, 0), half=0)
        b = place(w, 1, 0)
        arrived(w, b)
        push(w, 3, b, place(w, -1, 0), half=1)
    for n, s in ((1, 1), (2, -1)):
        for w in (0, 1):
            b = place(w, s, 0)
            push(w, 4 + 4 * n, b, place(w, 0, 1))
            push(w, 5 + 4 * n, b, place(w, 0, -1))
    for w in (0, 1):
        b = place(w, 2, 0)
        arrived(w, b, 0)
        arrived(w, b, 1)
        push(w, 16, b, place(w, 0, 1))
        push(w, 17, b, place(w, 0, -1))
    pass_on()
    for n, s in ((0, 0), (1, 1), (2, -1), (3, 2)):
        for w in (0, 1):
            b = place(w, s, -1)
            arrived(w, b)
            push(w, 6 + 4 * n, b, place(w, 0, 1), half=0)
            b = place(w, s, 1)
            arrived(w, b)
            push(w, 7 + 4 * n, b, place(w, 0, -1), half=1)
    for n, s in ((0, 0), (1, 1), (2, -1), (3, 2)):
        for w in (0, 1):
            b = place(w, s, 2)
            arrived(w, b, 0)
            arrived(w, b, 1)

    for r in range(CHUNKS):
        source, chunk = source_of(me, r)

        @pl.when(source != me)
        def _():
            for n in range(3):
                row_copy(n, 0, r, me).wait_recv()

        @pl.when(source == me)
        def _():
            for n in range(3):
                own_row(n, chunk, r).wait()

    for c in range(CHUNKS):
        @pl.when(taker_of(me, c) != me)
        def _():
            for n in range(3):
                row_copy(n, c, 0, me).wait_send()

    for side in range(2):
        for n in range(2):
            on_copy(n, side, 0, me).wait_send()
    for c in sent:
        c.wait_send()
    for c in own:
        c.wait()


def gather(k, v, q, do, o):
    anyspace = pl.BlockSpec(memory_space=pl.ANY)
    T = k.shape[0] * SENDERS
    sds = jax.ShapeDtypeStruct
    dma = pltpu.SemaphoreType.DMA
    de = (CHUNKS, 8, R)
    return pl.pallas_call(
        gather_kernel,
        out_shape=(sds((T, HD), k.dtype), sds((T, HD), k.dtype), sds(q.shape, q.dtype), sds(do.shape, do.dtype), sds(de, jnp.float32)),
        in_specs=[anyspace] * 5, out_specs=(anyspace,) * 5,
        scratch_shapes=[pltpu.VMEM(do.shape, do.dtype), pltpu.VMEM(o.shape, o.dtype), pltpu.VMEM(de, jnp.float32),
            pltpu.VMEM((2, 2) + q.shape[1:], q.dtype), dma((2, 20)), dma((2, SENDERS, 2)), dma((3, CHUNKS)), dma((3, CHUNKS)),
            dma((2, 2)), dma((2, 2)), dma((7,))],
        compiler_params=pltpu.CompilerParams(collective_id=0, has_side_effects=True, vmem_limit_bytes=60 * 2**20),
    )(k, v, q, do, o)


def reduce_kernel(dk_ref, dv_ref, dq_ref, dk_out, dv_out, dq_out, own, near, via, got, mid, via2, got2, hold,
                  send1, recv1, send2, recv2, row_send, row_recv, hop_recv, on_send, own_sem):
    me = lax.axis_index("ctx")
    y, x = me // SIDE, me % SIDE
    greet(me)
    HALF = BLOCK // 2
    refs = (dk_ref, dv_ref)
    outs = (dk_out, dv_out)
    sent = []

    def lane(w, leg):
        return (y, x)[(w + leg) % 2]

    def peer(w, leg, s):
        return at(y + s, x) if (w + leg) % 2 == 0 else at(y, x + s)

    def part(w, s, half):
        line = (lane(w, 0) + s + SIDE) % SIDE
        two = pl.ds(2 * half, 2)
        return refs[w].at[line, two] if w == 0 else refs[w].at[two, line]

    def push(src, dst, ssem, rsem, to):
        c = send(src, dst, ssem, rsem, to)
        c.start()
        sent.append(c)

    for w in (0, 1):
        up, down = peer(w, 0, 1), peer(w, 0, -1)
        push(part(w, 2, 0), via.at[w, 0], send1.at[w, 0], recv1.at[w, 0], up)
        push(part(w, 2, 1), via.at[w, 1], send1.at[w, 1], recv1.at[w, 1], down)
    for w in (0, 1):
        up, down = peer(w, 0, 1), peer(w, 0, -1)
        push(part(w, 1, 1), got.at[w, 0, 1], send1.at[w, 3], recv1.at[w, 3], up)
        push(part(w, -1, 0), got.at[w, 1, 0], send1.at[w, 4], recv1.at[w, 4], down)

    local = []
    for w in (0, 1):
        line = lane(w, 0)
        local.append(pltpu.make_async_copy(refs[w].at[line] if w == 0 else refs[w].at[:, line], own.at[w], own_sem.at[1 + 3 * w]))
        for d in (0, 1):
            local.append(pltpu.make_async_copy(part(w, 1 - 2 * d, d), near.at[w, d], own_sem.at[2 + 3 * w + d]))
    for c in local:
        c.start()

    def row_copy(r, c, to):
        return send(dq_ref.at[r], dq_out.at[c], row_send.at[r], row_recv.at[c], to)

    def hop_copy(r, side, to):
        return send(dq_ref.at[r], hold.at[side], row_send.at[r], hop_recv.at[side], to)

    def on_copy(side, c, to):
        return send(hold.at[side], dq_out.at[c], on_send.at[side], row_recv.at[c], to)

    def own_row(r, c):
        return pltpu.make_async_copy(dq_ref.at[r], dq_out.at[c], own_sem.at[0])

    def send_rows():
        for r in range(CHUNKS):
            to, c = source_of(me, r)
            opposite = r // 2 == (y + 2) % SIDE
            far = c % 2

            @pl.when(opposite & (far == 0))
            def _():
                hop_copy(r, 0, at(y + 1, x)).start()

            @pl.when(opposite & (far == 1))
            def _():
                hop_copy(r, 1, at(y - 1, to % SIDE)).start()

            @pl.when(jnp.logical_not(opposite) & (to != me))
            def _():
                row_copy(r, c, to).start()

            @pl.when(to == me)
            def _():
                own_row(r, c).start()

    def wait1(w, slot, dst):
        send(dst, dst, send1.at[w, slot], recv1.at[w, slot], me).wait_recv()

    def tile(i):
        return pl.ds(pl.multiple_of(i * 128, 128), 128)

    for w in (0, 1):
        for d in (0, 1):
            wait1(w, d, via.at[w, d])
            local[3 * w + 1 + d].wait()

            def add(i, _, w=w, d=d):
                r = tile(i)
                for b in range(2):
                    mine = near[w, d, b, r, :]
                    via[w, d, b, r, :] = (via[w, d, b, r, :].astype(jnp.float32) + mine.astype(jnp.float32)).astype(jnp.bfloat16)
                return 0
            lax.fori_loop(0, BLOCK // 128, add, 0)
            push(via.at[w, d], got.at[w, d, d], send1.at[w, 2 if d == 0 else 5], recv1.at[w, 2 if d == 0 else 5],
                 peer(w, 0, 1 if d == 0 else -1))

    send_rows()

    def pass_back():
        for side in range(2):
            owner = at(y + 1, x) if side == 0 else at(y - 1, x)
            taker = at(y - 1, x) if side == 0 else at(y + 1, jnp.where(x % 2 == 0, x - 1, x + 1))
            reverse = (owner // 2) % 2 == 1
            c = 2 * jnp.where(reverse, SIDE - 1 - taker // SIDE, taker // SIDE) + side
            hop_copy(0, side, me).wait_recv()
            on_copy(side, c, owner).start()

    for w in (0, 1):
        for slot, d, h in ((3, 0, 1), (4, 1, 0), (2, 0, 0), (5, 1, 1)):
            wait1(w, slot, got.at[w, d, h])
        local[3 * w].wait()

        def add4(i, _, w=w):
            r = tile(i)
            for b in range(SIDE):
                mine = own[w, b, r, :]
                total = mine.astype(jnp.float32) + got[w, 0, b // 2, b % 2, r, :].astype(jnp.float32)
                mid[w, b, r, :] = (total + got[w, 1, b // 2, b % 2, r, :].astype(jnp.float32)).astype(jnp.bfloat16)
            return 0
        lax.fori_loop(0, BLOCK // 128, add4, 0)

        def half2(s, h, w=w):
            return mid.at[w, (lane(w, 1) + s + SIDE) % SIDE, pl.ds(h * HALF, HALF)]
        up, down = peer(w, 1, 1), peer(w, 1, -1)
        push(half2(2, 0), via2.at[w, 0], send2.at[w, 0], recv2.at[w, 0], up)
        push(half2(2, 1), via2.at[w, 1], send2.at[w, 1], recv2.at[w, 1], down)
        push(half2(1, 1), got2.at[w, 0, 1], send2.at[w, 3], recv2.at[w, 3], up)
        push(half2(-1, 0), got2.at[w, 1, 0], send2.at[w, 4], recv2.at[w, 4], down)

    pass_back()

    def wait2(w, slot, dst):
        send(dst, dst, send2.at[w, slot], recv2.at[w, slot], me).wait_recv()

    for w in (0, 1):
        for d in (0, 1):
            wait2(w, d, via2.at[w, d])
            line = (lane(w, 1) + (1 if d == 0 else 3)) % SIDE
            for i in range(2):
                r = pl.ds(i * 128, 128)
                mine = mid[w, line, pl.ds(d * HALF + i * 128, 128), :]
                via2[w, d, r, :] = (via2[w, d, r, :].astype(jnp.float32) + mine.astype(jnp.float32)).astype(jnp.bfloat16)
            push(via2.at[w, d], got2.at[w, d, d], send2.at[w, 2 if d == 0 else 5], recv2.at[w, 2 if d == 0 else 5],
                 peer(w, 1, 1 if d == 0 else -1))
    for w in (0, 1):
        for slot, d, h in ((3, 0, 1), (4, 1, 0), (2, 0, 0), (5, 1, 1)):
            wait2(w, slot, got2.at[w, d, h])
        for h in (0, 1):
            for i in range(2):
                r = pl.ds(i * 128, 128)
                out = pl.ds(h * HALF + i * 128, 128)
                total = mid[w, lane(w, 1), out, :].astype(jnp.float32) + got2[w, 0, h, r, :].astype(jnp.float32)
                outs[w][out, :] = (total + got2[w, 1, h, r, :].astype(jnp.float32)).astype(jnp.bfloat16)
    for c in range(CHUNKS):
        @pl.when(taker_of(me, c) != me)
        def _():
            row_copy(0, c, me).wait_recv()

        @pl.when(taker_of(me, c) == me)
        def _():
            own_row(me // 2, c).wait()

    for r in range(CHUNKS):
        @pl.when(source_of(me, r)[0] != me)
        def _():
            row_copy(r, 0, me).wait_send()

    for side in range(2):
        on_copy(side, 0, me).wait_send()
    for c in sent:
        c.wait_send()


def reduce(dk, dv, dq):
    anyspace = pl.BlockSpec(memory_space=pl.ANY)
    vm = pl.BlockSpec(memory_space=pltpu.VMEM)
    sds = jax.ShapeDtypeStruct
    dma = pltpu.SemaphoreType.DMA
    bf = jnp.bfloat16
    half = BLOCK // 2
    shape = (SIDE, SIDE, BLOCK, HD)
    return pl.pallas_call(
        reduce_kernel,
        out_shape=(sds((BLOCK, HD), bf), sds((BLOCK, HD), bf), sds(dq.shape, bf)),
        in_specs=[anyspace] * 3, out_specs=(vm, vm, anyspace),
        scratch_shapes=[pltpu.VMEM((2, SIDE, BLOCK, HD), bf), pltpu.VMEM((2, 2, 2, BLOCK, HD), bf),
            pltpu.VMEM((2, 2, 2, BLOCK, HD), bf), pltpu.VMEM((2, 2, 2, 2, BLOCK, HD), bf), pltpu.VMEM((2, SIDE, BLOCK, HD), bf),
            pltpu.VMEM((2, 2, half, HD), bf), pltpu.VMEM((2, 2, 2, half, HD), bf), pltpu.VMEM((2,) + dq.shape[1:], bf),
            dma((2, 6)), dma((2, 6)), dma((2, 6)), dma((2, 6)), dma((CHUNKS,)), dma((CHUNKS,)), dma((2,)), dma((2,)), dma((7,))],
        compiler_params=pltpu.CompilerParams(collective_id=1, has_side_effects=True, vmem_limit_bytes=60 * 2**20),
    )(dk.reshape(shape), dv.reshape(shape), dq)


def on_device(queries, attn_keys, attn_values, attn_output, output_grad, chain_lens):
    me = lax.axis_index("ctx")
    lens = chain_lens[0].astype(jnp.int32)
    ends = jnp.stack([lens[0], lens[0] + lens[1], lens[0] + lens[1] + lens[2]])
    tiles = lambda a: a[0].reshape(CHUNKS, TP, -1)
    k, v, q, do, delta = gather(attn_keys[0], attn_values[0], tiles(queries), tiles(output_grad), tiles(attn_output))
    source, chunk = source_of(me, jnp.arange(CHUNKS, dtype=jnp.int32))
    base = source * BLOCK + chunk * TP
    dq, dk, dv = call(base, ends, q, do, delta, k, v)
    dk, dv, dq = reduce(dk, dv, dq)
    return dq.reshape(1, BLOCK, -1), dk[None], dv[None]


def solution(mesh):
    tok = P("grp", "ctx", None)
    return jax.shard_map(
        on_device,
        mesh=mesh,
        in_specs=(tok, tok, tok, tok, tok, P("grp", None)),
        out_specs=(tok, tok, tok),
        check_vma=False,
    )
```

```python
import functools, math
import jax, jax.numpy as jnp
from jax import lax
from jax.experimental import pallas as pl
from jax.experimental.pallas import tpu as pltpu
from jax.sharding import PartitionSpec as P

HD = 128
GQA = 8
BLOCK = 512
TP = 64
R = TP * GQA
SUB = 128
SB = 64
BIG = 1536
SCALE = HD ** -0.5
STEP = 256
C2 = SCALE * math.log2(math.e)
NN = (((1,), (0,)), ((), ()))


def dot(a, b):
    return lax.dot_general(a, b, NN, preferred_element_type=jnp.float32)


def kernel(lens_ref, q_any, do_any, delta_ref, k_ref, v_any, dq_any, dk_any, dv_any,
           kt, pbuf, mbuf, mrun, lrun, dka, dva, qs, dos, dqt, qst, dost, q_ref, do_ref, v_ref, dq_ref, dk_ref, dv_ref, in_sem, sem, out_sem):
    T = k_ref.shape[0]

    me = lax.axis_index("ctx")
    fetch = [pltpu.make_async_copy(src, dst, in_sem.at[n]) for n, (src, dst) in enumerate(((q_any, q_ref), (do_any, do_ref), (v_any, v_ref)))]
    for c in fetch:
        c.start()

    def init(i, _):
        rows = pl.ds(pl.multiple_of(i * 512, 512), 512)
        kt[:, rows] = k_ref[rows, :].T
        dka[rows, :] = jnp.zeros((512, HD), jnp.float32)
        dva[rows, :] = jnp.zeros((512, HD), jnp.float32)
        return 0
    lax.fori_loop(0, T // 512, init, 0)
    for c in fetch:
        c.wait()
    e0 = lens_ref[0, 0]
    e1 = e0 + lens_ref[0, 1]

    def dq_out(t):
        return pltpu.make_async_copy(dq_ref.at[t], dq_any.at[t], sem.at[t])

    def start_of(p):
        return jnp.where(p < e0, 0, jnp.where(p < e1, e0, e1))

    def tile(t, _):
        source, chunk = source_of(me, t)
        p0 = source * BLOCK + chunk * TP
        lo = (start_of(p0) // SUB) * SUB
        hi = ((p0 + TP + SUB - 1) // SUB) * SUB
        odd = (hi - lo) % STEP != 0
        hi = jnp.where(odd & (lo == 0), hi + SUB, hi)
        lo = jnp.where(odd & (lo > 0), lo - SUB, lo)
        nb = (hi - lo) // BIG
        rest = (hi - lo) - nb * BIG
        for h in range(GQA):
            qs[h * TP:(h + 1) * TP, :] = q_ref[t, :, h * HD:(h + 1) * HD]
            dos[h * TP:(h + 1) * TP, :] = do_ref[t, :, h * HD:(h + 1) * HD]
        qst[...] = qs[...].T
        dost[...] = dos[...].T
        rpos = p0 + lax.broadcasted_iota(jnp.int32, (1, R), 1) % TP
        rstart = start_of(rpos)
        last_start = start_of(p0 + TP - 1)

        def stats(first, size, masked):
            first = pl.multiple_of(first, SUB)
            s = dot(k_ref[pl.ds(first, size), :], qst[...])
            if masked:
                spos = first + lax.broadcasted_iota(jnp.int32, (size, 1), 0)
                s = jnp.where((spos >= rstart) & (spos <= rpos), s, -1e30)
            s = s.reshape(size // SB, SB // 8, 8, R)
            m = jnp.max(s, axis=1)
            p = jnp.exp2((s - m[:, None]) * C2)
            pbuf[pl.ds(first, size), :] = p.reshape(size, R)
            mbuf[pl.ds(first // SB, size // SB)] = m
            old = mrun[...]
            new = jnp.maximum(old, jnp.max(m, axis=0))
            lrun[...] = lrun[...] * jnp.exp2((old - new) * C2) + jnp.sum(jnp.sum(p, axis=1) * jnp.exp2((m - new) * C2), axis=0)
            mrun[...] = new

        def grads(first, size):
            first = pl.multiple_of(first, SUB)
            rows = pl.ds(first, size)
            f = jnp.exp2((mbuf[pl.ds(first // SB, size // SB)] - top) * C2) * linv
            p = (pbuf[rows, :].reshape(size // SB, SB // 8, 8, R) * f[:, None]).reshape(size, R)
            dp = dot(v_ref[rows, :], dost[...])
            ds = (p * (dp - delta)).astype(jnp.bfloat16)
            dva[rows, :] += dot(p.astype(jnp.bfloat16), dos[...])
            dka[rows, :] += dot(ds, qs[...])
            dqt[...] += dot(kt[:, rows], ds)

        def sweep(body, last):
            def big(j, _):
                body(lo + j * BIG, BIG)
                return 0
            lax.fori_loop(0, nb, big, 0)
            at = lo + nb * BIG
            for size in range(STEP, BIG, STEP):
                pl.when(rest == size)(functools.partial(last, at, size))

        def stats_any(first, size):
            need = (first < last_start) | (first + size - 1 > p0)
            pl.when(need)(lambda: stats(first, size, True))
            pl.when(jnp.logical_not(need))(lambda: stats(first, size, False))
        mrun[...] = jnp.full((8, R), -1e30, jnp.float32)
        lrun[...] = jnp.zeros((8, R), jnp.float32)
        sweep(stats_any, functools.partial(stats, masked=True))
        top = jnp.max(mrun[...], axis=0, keepdims=True)
        linv = 1.0 / jnp.sum(lrun[...] * jnp.exp2((mrun[...] - top) * C2), axis=0, keepdims=True)
        delta = delta_ref[t, 0:1, :]
        dqt[...] = jnp.zeros((HD, R), jnp.float32)
        sweep(grads, grads)
        dq = (dqt[...].T * SCALE).astype(jnp.bfloat16)
        for h in range(GQA):
            dq_ref[t, :, h * HD:(h + 1) * HD] = dq[h * TP:(h + 1) * TP, :]
        dq_out(t).start()
        return 0
    lax.fori_loop(0, q_ref.shape[0], tile, 0)

    def part_out(i, n):
        rows = pl.ds(pl.multiple_of(i * 1024, 1024), 1024)
        src, dst = ((dk_ref, dk_any), (dv_ref, dv_any))[n]
        return pltpu.make_async_copy(src.at[rows], dst.at[rows], out_sem.at[n, i])

    def fin(i, _):
        rows = pl.ds(pl.multiple_of(i * 1024, 1024), 1024)
        dk_ref[rows, :] = (dka[rows, :] * SCALE).astype(dk_ref.dtype)
        dv_ref[rows, :] = dva[rows, :].astype(dv_ref.dtype)
        part_out(i, 0).start()
        part_out(i, 1).start()
        return 0
    lax.fori_loop(0, T // 1024, fin, 0)

    def drain(i, _):
        part_out(i, 0).wait()
        part_out(i, 1).wait()
        return 0
    lax.fori_loop(0, T // 1024, drain, 0)

    def drain_q(t, _):
        dq_out(t).wait()
        return 0
    lax.fori_loop(0, q_ref.shape[0], drain_q, 0)


def call(lens, q, do, delta, k, v):
    T = k.shape[0]
    vm = pl.BlockSpec(memory_space=pltpu.VMEM)
    sm = pl.BlockSpec(memory_space=pltpu.SMEM)
    hbm = pl.BlockSpec(memory_space=pl.ANY)
    f32 = jnp.float32
    bf = jnp.bfloat16
    return pl.pallas_call(
        kernel,
        out_shape=(jax.ShapeDtypeStruct(q.shape, bf), jax.ShapeDtypeStruct((T, HD), bf), jax.ShapeDtypeStruct((T, HD), bf)),
        in_specs=[sm, hbm, hbm, vm, vm, hbm],
        out_specs=(hbm, hbm, hbm),
        scratch_shapes=[pltpu.VMEM((HD, T), bf), pltpu.VMEM((T, R), f32), pltpu.VMEM((T // SB, 8, R), f32), pltpu.VMEM((8, R), f32), pltpu.VMEM((8, R), f32),
            pltpu.VMEM((T, HD), f32), pltpu.VMEM((T, HD), f32), pltpu.VMEM((R, HD), bf), pltpu.VMEM((R, HD), bf), pltpu.VMEM((HD, R), f32),
            pltpu.VMEM((HD, R), bf), pltpu.VMEM((HD, R), bf),
            pltpu.VMEM(q.shape, bf), pltpu.VMEM(q.shape, bf), pltpu.VMEM((T, HD), bf), pltpu.VMEM(q.shape, bf), pltpu.VMEM((T, HD), bf), pltpu.VMEM((T, HD), bf),
            pltpu.SemaphoreType.DMA((3,)), pltpu.SemaphoreType.DMA((q.shape[0],)), pltpu.SemaphoreType.DMA((2, T // 1024))],
        compiler_params=pltpu.CompilerParams(vmem_limit_bytes=60 * 2**20),
    )(lens, q, do, delta, k, v)


MESH = pl.DeviceIdType.MESH
SIDE = 4
SENDERS = SIDE * SIDE
CHUNKS = 8


def source_of(dev, r):
    y, x = dev // SIDE, dev % SIDE
    ahead = (x - 2 * (r % 2) + SIDE) % SIDE
    upper = jnp.where((ahead == 1) | (ahead == 2), 1, 0)
    far = jnp.where(ahead >= 2, 1, 0)
    return 2 * r + upper, 2 * y + far


def taker_of(owner, c):
    r, upper, far = owner // 2, owner % 2, c % 2
    x = (2 * (r % 2) + jnp.where(upper == 1, 1 + far, SIDE - far)) % SIDE
    return c // 2 * SIDE + x


def at(y, x):
    return (y + SIDE) % SIDE * SIDE + (x + SIDE) % SIDE


def greet(me):
    barrier = pltpu.get_barrier_semaphore()
    for step in range(1, SENDERS):
        pl.semaphore_signal(barrier, inc=1, device_id={"ctx": (me + step) % SENDERS}, device_id_type=MESH)
    pl.semaphore_wait(barrier, SENDERS - 1)


def send(src, dst, send_sem, recv_sem, to):
    return pltpu.make_async_remote_copy(
        src_ref=src, dst_ref=dst, send_sem=send_sem, recv_sem=recv_sem, device_id={"ctx": to}, device_id_type=MESH)


def gather_kernel(k_ref, v_ref, q_ref, do_ref, o_ref, k_all, v_all, q_out, do_out, de_out,
                  do_v, o_v, de_ref, hold, kv_send, kv_recv, row_send, row_recv, hop_recv, on_send, own_sem):
    me = lax.axis_index("ctx")
    y, x = me // SIDE, me % SIDE
    fetch = [pltpu.make_async_copy(do_ref, do_v, own_sem.at[5]), pltpu.make_async_copy(o_ref, o_v, own_sem.at[6])]
    for c in fetch:
        c.start()
    greet(me)
    HALF = BLOCK // 2

    def block(which, i, half=None):
        first, size = (i * BLOCK, BLOCK) if half is None else (i * BLOCK + half * HALF, HALF)
        return (k_all, v_all)[which].at[pl.ds(pl.multiple_of(first, HALF), size)]

    sent = []

    def push(which, slot, owner, to, half=None, src=None):
        c = send(block(which, owner, half) if src is None else src, block(which, owner, half),
                 kv_send.at[which, slot], kv_recv.at[which, owner, 0 if half is None else half], to)
        c.start()
        sent.append(c)

    def arrived(which, owner, half=None):
        b = block(which, owner, half)
        send(b, b, kv_send.at[which, 0], kv_recv.at[which, owner, 0 if half is None else half], me).wait_recv()

    def place(which, first, second):
        return at(y + second, x + first) if which == 0 else at(y + first, x + second)

    own = [pltpu.make_async_copy(ref, block(w, me), own_sem.at[w]) for w, ref in ((0, k_ref), (1, v_ref))]
    for w, ref in ((0, k_ref), (1, v_ref)):
        push(w, 0, me, place(w, 1, 0), src=ref)
        push(w, 1, me, place(w, -1, 0), src=ref)
    for w, ref in ((0, k_ref), (1, v_ref)):
        push(w, 4, me, place(w, 0, 1), src=ref)
        push(w, 5, me, place(w, 0, -1), src=ref)
    for c in own:
        c.start()

    rows = ((q_ref, q_out), (do_ref, do_out), (de_ref, de_out))

    def row_copy(n, c, r, to):
        src, dst = rows[n]
        return send(src.at[c], dst.at[r], row_send.at[n, c], row_recv.at[n, r], to)

    def hop_copy(n, c, side, to):
        return send(rows[n][0].at[c], hold.at[n, side], row_send.at[n, c], hop_recv.at[n, side], to)

    def on_copy(n, side, r, to):
        return send(hold.at[n, side], rows[n][1].at[r], on_send.at[n, side], row_recv.at[n, r], to)

    def own_row(n, c, r):
        src, dst = rows[n]
        return pltpu.make_async_copy(src.at[c], dst.at[r], own_sem.at[2 + n])

    def send_rows():
        for c in range(CHUNKS):
            to = taker_of(me, c)
            opposite = to // SIDE == (y + 2) % SIDE
            side = c % 2

            @pl.when(opposite)
            def _():
                hop = at(y + 1, x) if side == 0 else at(y - 1, to % SIDE)
                for n in range(2):
                    hop_copy(n, c, side, hop).start()

            @pl.when(jnp.logical_not(opposite) & (to != me))
            def _():
                for n in range(2):
                    row_copy(n, c, me // 2, to).start()

            @pl.when(to == me)
            def _():
                for n in range(2):
                    own_row(n, c, me // 2).start()

    def send_deltas():
        for c in fetch:
            c.wait()
        ones = jnp.ones((8, HD), jnp.float32)

        def chunk(c, _):
            for h in range(GQA):
                lanes = slice(h * HD, (h + 1) * HD)
                prod = do_v[c, :, lanes].astype(jnp.float32) * o_v[c, :, lanes].astype(jnp.float32)
                de_ref[c, :, h * TP:(h + 1) * TP] = lax.dot_general(
                    ones, prod, (((1,), (1,)), ((), ())), precision=lax.Precision.HIGHEST, preferred_element_type=jnp.float32)
            return 0
        lax.fori_loop(0, CHUNKS, chunk, 0)
        for c in range(CHUNKS):
            to = taker_of(me, c)

            @pl.when(to != me)
            def _():
                row_copy(2, c, me // 2, to).start()

            @pl.when(to == me)
            def _():
                own_row(2, c, me // 2).start()

    def pass_on():
        for side in range(2):
            owner = at(y - 1, x) if side == 0 else at(y + 1, jnp.where(x % 2 == 1, x + 1, x - 1))
            to = at(y + 1, x) if side == 0 else at(y - 1, x)
            for n in range(2):
                hop_copy(n, 0, side, me).wait_recv()
                on_copy(n, side, owner // 2, to).start()

    send_rows()
    send_deltas()
    for w in (0, 1):
        b = place(w, -1, 0)
        arrived(w, b)
        push(w, 2, b, place(w, 1, 0), half=0)
        b = place(w, 1, 0)
        arrived(w, b)
        push(w, 3, b, place(w, -1, 0), half=1)
    for n, s in ((1, 1), (2, -1)):
        for w in (0, 1):
            b = place(w, s, 0)
            push(w, 4 + 4 * n, b, place(w, 0, 1))
            push(w, 5 + 4 * n, b, place(w, 0, -1))
    for w in (0, 1):
        b = place(w, 2, 0)
        arrived(w, b, 0)
        arrived(w, b, 1)
        push(w, 16, b, place(w, 0, 1))
        push(w, 17, b, place(w, 0, -1))
    pass_on()
    for n, s in ((0, 0), (1, 1), (2, -1), (3, 2)):
        for w in (0, 1):
            b = place(w, s, -1)
            arrived(w, b)
            push(w, 6 + 4 * n, b, place(w, 0, 1), half=0)
            b = place(w, s, 1)
            arrived(w, b)
            push(w, 7 + 4 * n, b, place(w, 0, -1), half=1)
    for n, s in ((0, 0), (1, 1), (2, -1), (3, 2)):
        for w in (0, 1):
            b = place(w, s, 2)
            arrived(w, b, 0)
            arrived(w, b, 1)

    for r in range(CHUNKS):
        source, chunk = source_of(me, r)

        @pl.when(source != me)
        def _():
            for n in range(3):
                row_copy(n, 0, r, me).wait_recv()

        @pl.when(source == me)
        def _():
            for n in range(3):
                own_row(n, chunk, r).wait()

    for c in range(CHUNKS):
        @pl.when(taker_of(me, c) != me)
        def _():
            for n in range(3):
                row_copy(n, c, 0, me).wait_send()

    for side in range(2):
        for n in range(2):
            on_copy(n, side, 0, me).wait_send()
    for c in sent:
        c.wait_send()
    for c in own:
        c.wait()


def gather(k, v, q, do, o):
    anyspace = pl.BlockSpec(memory_space=pl.ANY)
    T = k.shape[0] * SENDERS
    sds = jax.ShapeDtypeStruct
    dma = pltpu.SemaphoreType.DMA
    de = (CHUNKS, 8, R)
    return pl.pallas_call(
        gather_kernel,
        out_shape=(sds((T, HD), k.dtype), sds((T, HD), k.dtype), sds(q.shape, q.dtype), sds(do.shape, do.dtype), sds(de, jnp.float32)),
        in_specs=[anyspace] * 5, out_specs=(anyspace,) * 5,
        scratch_shapes=[pltpu.VMEM(do.shape, do.dtype), pltpu.VMEM(o.shape, o.dtype), pltpu.VMEM(de, jnp.float32),
            pltpu.VMEM((2, 2) + q.shape[1:], q.dtype), dma((2, 20)), dma((2, SENDERS, 2)), dma((3, CHUNKS)), dma((3, CHUNKS)),
            dma((2, 2)), dma((2, 2)), dma((7,))],
        compiler_params=pltpu.CompilerParams(collective_id=0, has_side_effects=True, vmem_limit_bytes=60 * 2**20),
    )(k, v, q, do, o)


def reduce_kernel(dk_ref, dv_ref, dq_ref, dk_out, dv_out, dq_out, own, near, via, got, mid, via2, got2, hold,
                  send1, recv1, send2, recv2, row_send, row_recv, hop_recv, on_send, own_sem):
    me = lax.axis_index("ctx")
    y, x = me // SIDE, me % SIDE
    greet(me)
    HALF = BLOCK // 2
    refs = (dk_ref, dv_ref)
    outs = (dk_out, dv_out)
    sent = []

    def lane(w, leg):
        return (y, x)[(w + leg) % 2]

    def peer(w, leg, s):
        return at(y + s, x) if (w + leg) % 2 == 0 else at(y, x + s)

    def part(w, s, half):
        line = (lane(w, 0) + s + SIDE) % SIDE
        two = pl.ds(2 * half, 2)
        return refs[w].at[line, two] if w == 0 else refs[w].at[two, line]

    def push(src, dst, ssem, rsem, to):
        c = send(src, dst, ssem, rsem, to)
        c.start()
        sent.append(c)

    for w in (0, 1):
        up, down = peer(w, 0, 1), peer(w, 0, -1)
        push(part(w, 2, 0), via.at[w, 0], send1.at[w, 0], recv1.at[w, 0], up)
        push(part(w, 2, 1), via.at[w, 1], send1.at[w, 1], recv1.at[w, 1], down)
    for w in (0, 1):
        up, down = peer(w, 0, 1), peer(w, 0, -1)
        push(part(w, 1, 1), got.at[w, 0, 1], send1.at[w, 3], recv1.at[w, 3], up)
        push(part(w, -1, 0), got.at[w, 1, 0], send1.at[w, 4], recv1.at[w, 4], down)

    local = []
    for w in (0, 1):
        line = lane(w, 0)
        local.append(pltpu.make_async_copy(refs[w].at[line] if w == 0 else refs[w].at[:, line], own.at[w], own_sem.at[1 + 3 * w]))
        for d in (0, 1):
            local.append(pltpu.make_async_copy(part(w, 1 - 2 * d, d), near.at[w, d], own_sem.at[2 + 3 * w + d]))
    for c in local:
        c.start()

    def row_copy(r, c, to):
        return send(dq_ref.at[r], dq_out.at[c], row_send.at[r], row_recv.at[c], to)

    def hop_copy(r, side, to):
        return send(dq_ref.at[r], hold.at[side], row_send.at[r], hop_recv.at[side], to)

    def on_copy(side, c, to):
        return send(hold.at[side], dq_out.at[c], on_send.at[side], row_recv.at[c], to)

    def own_row(r, c):
        return pltpu.make_async_copy(dq_ref.at[r], dq_out.at[c], own_sem.at[0])

    def send_rows():
        for r in range(CHUNKS):
            to, c = source_of(me, r)
            opposite = r // 2 == (y + 2) % SIDE
            far = c % 2

            @pl.when(opposite & (far == 0))
            def _():
                hop_copy(r, 0, at(y + 1, x)).start()

            @pl.when(opposite & (far == 1))
            def _():
                hop_copy(r, 1, at(y - 1, to % SIDE)).start()

            @pl.when(jnp.logical_not(opposite) & (to != me))
            def _():
                row_copy(r, c, to).start()

            @pl.when(to == me)
            def _():
                own_row(r, c).start()

    def wait1(w, slot, dst):
        send(dst, dst, send1.at[w, slot], recv1.at[w, slot], me).wait_recv()

    def tile(i):
        return pl.ds(pl.multiple_of(i * 128, 128), 128)

    for w in (0, 1):
        for d in (0, 1):
            wait1(w, d, via.at[w, d])
            local[3 * w + 1 + d].wait()

            def add(i, _, w=w, d=d):
                r = tile(i)
                for b in range(2):
                    mine = near[w, d, b, r, :]
                    via[w, d, b, r, :] = (via[w, d, b, r, :].astype(jnp.float32) + mine.astype(jnp.float32)).astype(jnp.bfloat16)
                return 0
            lax.fori_loop(0, BLOCK // 128, add, 0)
            push(via.at[w, d], got.at[w, d, d], send1.at[w, 2 if d == 0 else 5], recv1.at[w, 2 if d == 0 else 5],
                 peer(w, 0, 1 if d == 0 else -1))

    send_rows()

    def pass_back():
        for side in range(2):
            owner = at(y + 1, x) if side == 0 else at(y - 1, x)
            taker = at(y - 1, x) if side == 0 else at(y + 1, jnp.where(x % 2 == 0, x - 1, x + 1))
            c = 2 * (taker // SIDE) + side
            hop_copy(0, side, me).wait_recv()
            on_copy(side, c, owner).start()

    for w in (0, 1):
        for slot, d, h in ((3, 0, 1), (4, 1, 0), (2, 0, 0), (5, 1, 1)):
            wait1(w, slot, got.at[w, d, h])
        local[3 * w].wait()

        def add4(i, _, w=w):
            r = tile(i)
            for b in range(SIDE):
                mine = own[w, b, r, :]
                total = mine.astype(jnp.float32) + got[w, 0, b // 2, b % 2, r, :].astype(jnp.float32)
                mid[w, b, r, :] = (total + got[w, 1, b // 2, b % 2, r, :].astype(jnp.float32)).astype(jnp.bfloat16)
            return 0
        lax.fori_loop(0, BLOCK // 128, add4, 0)

        def half2(s, h, w=w):
            return mid.at[w, (lane(w, 1) + s + SIDE) % SIDE, pl.ds(h * HALF, HALF)]
        up, down = peer(w, 1, 1), peer(w, 1, -1)
        push(half2(2, 0), via2.at[w, 0], send2.at[w, 0], recv2.at[w, 0], up)
        push(half2(2, 1), via2.at[w, 1], send2.at[w, 1], recv2.at[w, 1], down)
        push(half2(1, 1), got2.at[w, 0, 1], send2.at[w, 3], recv2.at[w, 3], up)
        push(half2(-1, 0), got2.at[w, 1, 0], send2.at[w, 4], recv2.at[w, 4], down)

    pass_back()

    def wait2(w, slot, dst):
        send(dst, dst, send2.at[w, slot], recv2.at[w, slot], me).wait_recv()

    for w in (0, 1):
        for d in (0, 1):
            wait2(w, d, via2.at[w, d])
            line = (lane(w, 1) + (1 if d == 0 else 3)) % SIDE
            for i in range(2):
                r = pl.ds(i * 128, 128)
                mine = mid[w, line, pl.ds(d * HALF + i * 128, 128), :]
                via2[w, d, r, :] = (via2[w, d, r, :].astype(jnp.float32) + mine.astype(jnp.float32)).astype(jnp.bfloat16)
            push(via2.at[w, d], got2.at[w, d, d], send2.at[w, 2 if d == 0 else 5], recv2.at[w, 2 if d == 0 else 5],
                 peer(w, 1, 1 if d == 0 else -1))
    for w in (0, 1):
        for slot, d, h in ((3, 0, 1), (4, 1, 0), (2, 0, 0), (5, 1, 1)):
            wait2(w, slot, got2.at[w, d, h])
        for h in (0, 1):
            for i in range(2):
                r = pl.ds(i * 128, 128)
                out = pl.ds(h * HALF + i * 128, 128)
                total = mid[w, lane(w, 1), out, :].astype(jnp.float32) + got2[w, 0, h, r, :].astype(jnp.float32)
                outs[w][out, :] = (total + got2[w, 1, h, r, :].astype(jnp.float32)).astype(jnp.bfloat16)
    for c in range(CHUNKS):
        @pl.when(taker_of(me, c) != me)
        def _():
            row_copy(0, c, me).wait_recv()

        @pl.when(taker_of(me, c) == me)
        def _():
            own_row(me // 2, c).wait()

    for r in range(CHUNKS):
        @pl.when(source_of(me, r)[0] != me)
        def _():
            row_copy(r, 0, me).wait_send()

    for side in range(2):
        on_copy(side, 0, me).wait_send()
    for c in sent:
        c.wait_send()


def reduce(dk, dv, dq):
    anyspace = pl.BlockSpec(memory_space=pl.ANY)
    vm = pl.BlockSpec(memory_space=pltpu.VMEM)
    sds = jax.ShapeDtypeStruct
    dma = pltpu.SemaphoreType.DMA
    bf = jnp.bfloat16
    half = BLOCK // 2
    shape = (SIDE, SIDE, BLOCK, HD)
    return pl.pallas_call(
        reduce_kernel,
        out_shape=(sds((BLOCK, HD), bf), sds((BLOCK, HD), bf), sds(dq.shape, bf)),
        in_specs=[anyspace] * 3, out_specs=(vm, vm, anyspace),
        scratch_shapes=[pltpu.VMEM((2, SIDE, BLOCK, HD), bf), pltpu.VMEM((2, 2, 2, BLOCK, HD), bf),
            pltpu.VMEM((2, 2, 2, BLOCK, HD), bf), pltpu.VMEM((2, 2, 2, 2, BLOCK, HD), bf), pltpu.VMEM((2, SIDE, BLOCK, HD), bf),
            pltpu.VMEM((2, 2, half, HD), bf), pltpu.VMEM((2, 2, 2, half, HD), bf), pltpu.VMEM((2,) + dq.shape[1:], bf),
            dma((2, 6)), dma((2, 6)), dma((2, 6)), dma((2, 6)), dma((CHUNKS,)), dma((CHUNKS,)), dma((2,)), dma((2,)), dma((7,))],
        compiler_params=pltpu.CompilerParams(collective_id=1, has_side_effects=True, vmem_limit_bytes=60 * 2**20),
    )(dk.reshape(shape), dv.reshape(shape), dq)


def on_device(queries, attn_keys, attn_values, attn_output, output_grad, chain_lens):
    tiles = lambda a: a[0].reshape(CHUNKS, TP, -1)
    k, v, q, do, delta = gather(attn_keys[0], attn_values[0], tiles(queries), tiles(output_grad), tiles(attn_output))
    dq, dk, dv = call(chain_lens, q, do, delta, k, v)
    dk, dv, dq = reduce(dk, dv, dq)
    return dq.reshape(1, BLOCK, -1), dk[None], dv[None]


def solution(mesh):
    tok = P("grp", "ctx", None)
    return jax.shard_map(
        on_device,
        mesh=mesh,
        in_specs=(tok, tok, tok, tok, tok, P("grp", None)),
        out_specs=(tok, tok, tok),
        check_vma=False,
    )
```

```python
import functools, math
import jax, jax.numpy as jnp
from jax import lax
from jax.experimental import pallas as pl
from jax.experimental.pallas import tpu as pltpu
from jax.sharding import PartitionSpec as P

HD = 128
GQA = 8
BLOCK = 512
TP = 64
R = TP * GQA
SUB = 128
SB = 64
BIG = 1536
GCH = 256
SCALE = HD ** -0.5
STEP = 256
C2 = SCALE * math.log2(math.e)
NN = (((1,), (0,)), ((), ()))


def dot(a, b):
    return lax.dot_general(a, b, NN, preferred_element_type=jnp.float32)


def kernel(lens_ref, q_any, do_any, delta_ref, k_ref, v_any, dq_any, dk_any, dv_any,
           kt, pbuf, mbuf, mrun, lrun, dka, dva, qs, dos, dqt, qst, dost, q_ref, do_ref, v_ref, dq_ref, dk_ref, dv_ref, in_sem, sem, out_sem):
    T = k_ref.shape[0]

    me = lax.axis_index("ctx")
    fetch = [pltpu.make_async_copy(src, dst, in_sem.at[n]) for n, (src, dst) in enumerate(((q_any, q_ref), (do_any, do_ref), (v_any, v_ref)))]
    for c in fetch:
        c.start()

    def init(i, _):
        rows = pl.ds(pl.multiple_of(i * 512, 512), 512)
        kt[:, rows] = k_ref[rows, :].T
        dka[rows, :] = jnp.zeros((512, HD), jnp.float32)
        dva[rows, :] = jnp.zeros((512, HD), jnp.float32)
        return 0
    lax.fori_loop(0, T // 512, init, 0)
    for c in fetch:
        c.wait()
    e0 = lens_ref[0, 0]
    e1 = e0 + lens_ref[0, 1]

    def dq_out(t):
        return pltpu.make_async_copy(dq_ref.at[t], dq_any.at[t], sem.at[t])

    def start_of(p):
        return jnp.where(p < e0, 0, jnp.where(p < e1, e0, e1))

    def tile(t, _):
        source, chunk = source_of(me, t)
        p0 = source * BLOCK + chunk * TP
        lo = (start_of(p0) // SUB) * SUB
        hi = ((p0 + TP + SUB - 1) // SUB) * SUB
        odd = (hi - lo) % STEP != 0
        hi = jnp.where(odd & (lo == 0), hi + SUB, hi)
        lo = jnp.where(odd & (lo > 0), lo - SUB, lo)
        nb = (hi - lo) // BIG
        rest = (hi - lo) - nb * BIG
        for h in range(GQA):
            qs[h * TP:(h + 1) * TP, :] = q_ref[t, :, h * HD:(h + 1) * HD]
            dos[h * TP:(h + 1) * TP, :] = do_ref[t, :, h * HD:(h + 1) * HD]
        qst[...] = qs[...].T
        dost[...] = dos[...].T
        rpos = p0 + lax.broadcasted_iota(jnp.int32, (1, R), 1) % TP
        rstart = start_of(rpos)
        last_start = start_of(p0 + TP - 1)

        def stats(first, size, masked):
            first = pl.multiple_of(first, SUB)
            s = dot(k_ref[pl.ds(first, size), :], qst[...])
            if masked:
                spos = first + lax.broadcasted_iota(jnp.int32, (size, 1), 0)
                s = jnp.where((spos >= rstart) & (spos <= rpos), s, -1e30)
            s = s.reshape(size // SB, SB // 8, 8, R)
            m = jnp.max(s, axis=1)
            p = jnp.exp2((s - m[:, None]) * C2)
            pbuf[pl.ds(first, size), :] = p.reshape(size, R)
            mbuf[pl.ds(first // SB, size // SB)] = m
            old = mrun[...]
            new = jnp.maximum(old, jnp.max(m, axis=0))
            lrun[...] = lrun[...] * jnp.exp2((old - new) * C2) + jnp.sum(jnp.sum(p, axis=1) * jnp.exp2((m - new) * C2), axis=0)
            mrun[...] = new

        def grads(first, size):
            first = pl.multiple_of(first, SUB)
            dss = []
            for c in range(size // GCH):
                here = pl.multiple_of(first + c * GCH, SUB)
                rows = pl.ds(here, GCH)
                f = jnp.exp2((mbuf[pl.ds(here // SB, GCH // SB)] - top) * C2) * linv
                p = (pbuf[rows, :].reshape(GCH // SB, SB // 8, 8, R) * f[:, None]).reshape(GCH, R)
                dp = dot(v_ref[rows, :], dost[...])
                dss.append((p * (dp - delta)).astype(jnp.bfloat16))
                dva[rows, :] += dot(p.astype(jnp.bfloat16), dos[...])
                dka[rows, :] += dot(dss[-1], qs[...])
            dqt[...] += dot(kt[:, pl.ds(first, size)], jnp.concatenate(dss, axis=0))

        def sweep(body, last):
            def big(j, _):
                body(lo + j * BIG, BIG)
                return 0
            lax.fori_loop(0, nb, big, 0)
            at = lo + nb * BIG
            for size in range(STEP, BIG, STEP):
                pl.when(rest == size)(functools.partial(last, at, size))

        def stats_any(first, size):
            need = (first < last_start) | (first + size - 1 > p0)
            pl.when(need)(lambda: stats(first, size, True))
            pl.when(jnp.logical_not(need))(lambda: stats(first, size, False))
        mrun[...] = jnp.full((8, R), -1e30, jnp.float32)
        lrun[...] = jnp.zeros((8, R), jnp.float32)
        sweep(stats_any, functools.partial(stats, masked=True))
        top = jnp.max(mrun[...], axis=0, keepdims=True)
        linv = 1.0 / jnp.sum(lrun[...] * jnp.exp2((mrun[...] - top) * C2), axis=0, keepdims=True)
        delta = delta_ref[t, 0:1, :]
        dqt[...] = jnp.zeros((HD, R), jnp.float32)
        sweep(grads, grads)
        dq = (dqt[...].T * SCALE).astype(jnp.bfloat16)
        for h in range(GQA):
            dq_ref[t, :, h * HD:(h + 1) * HD] = dq[h * TP:(h + 1) * TP, :]
        dq_out(t).start()
        return 0
    lax.fori_loop(0, q_ref.shape[0], tile, 0)

    def part_out(i, n):
        rows = pl.ds(pl.multiple_of(i * 1024, 1024), 1024)
        src, dst = ((dk_ref, dk_any), (dv_ref, dv_any))[n]
        return pltpu.make_async_copy(src.at[rows], dst.at[rows], out_sem.at[n, i])

    def fin(i, _):
        rows = pl.ds(pl.multiple_of(i * 1024, 1024), 1024)
        dk_ref[rows, :] = (dka[rows, :] * SCALE).astype(dk_ref.dtype)
        dv_ref[rows, :] = dva[rows, :].astype(dv_ref.dtype)
        part_out(i, 0).start()
        part_out(i, 1).start()
        return 0
    lax.fori_loop(0, T // 1024, fin, 0)

    def drain(i, _):
        part_out(i, 0).wait()
        part_out(i, 1).wait()
        return 0
    lax.fori_loop(0, T // 1024, drain, 0)

    def drain_q(t, _):
        dq_out(t).wait()
        return 0
    lax.fori_loop(0, q_ref.shape[0], drain_q, 0)


def call(lens, q, do, delta, k, v):
    T = k.shape[0]
    vm = pl.BlockSpec(memory_space=pltpu.VMEM)
    sm = pl.BlockSpec(memory_space=pltpu.SMEM)
    hbm = pl.BlockSpec(memory_space=pl.ANY)
    f32 = jnp.float32
    bf = jnp.bfloat16
    return pl.pallas_call(
        kernel,
        out_shape=(jax.ShapeDtypeStruct(q.shape, bf), jax.ShapeDtypeStruct((T, HD), bf), jax.ShapeDtypeStruct((T, HD), bf)),
        in_specs=[sm, hbm, hbm, vm, vm, hbm],
        out_specs=(hbm, hbm, hbm),
        scratch_shapes=[pltpu.VMEM((HD, T), bf), pltpu.VMEM((T, R), f32), pltpu.VMEM((T // SB, 8, R), f32), pltpu.VMEM((8, R), f32), pltpu.VMEM((8, R), f32),
            pltpu.VMEM((T, HD), f32), pltpu.VMEM((T, HD), f32), pltpu.VMEM((R, HD), bf), pltpu.VMEM((R, HD), bf), pltpu.VMEM((HD, R), f32),
            pltpu.VMEM((HD, R), bf), pltpu.VMEM((HD, R), bf),
            pltpu.VMEM(q.shape, bf), pltpu.VMEM(q.shape, bf), pltpu.VMEM((T, HD), bf), pltpu.VMEM(q.shape, bf), pltpu.VMEM((T, HD), bf), pltpu.VMEM((T, HD), bf),
            pltpu.SemaphoreType.DMA((3,)), pltpu.SemaphoreType.DMA((q.shape[0],)), pltpu.SemaphoreType.DMA((2, T // 1024))],
        compiler_params=pltpu.CompilerParams(vmem_limit_bytes=60 * 2**20),
    )(lens, q, do, delta, k, v)


MESH = pl.DeviceIdType.MESH
SIDE = 4
SENDERS = SIDE * SIDE
CHUNKS = 8


def source_of(dev, r):
    y, x = dev // SIDE, dev % SIDE
    ahead = (x - 2 * (r % 2) + SIDE) % SIDE
    upper = jnp.where((ahead == 1) | (ahead == 2), 1, 0)
    far = jnp.where(ahead >= 2, 1, 0)
    return 2 * r + upper, 2 * y + far


def taker_of(owner, c):
    r, upper, far = owner // 2, owner % 2, c % 2
    x = (2 * (r % 2) + jnp.where(upper == 1, 1 + far, SIDE - far)) % SIDE
    return c // 2 * SIDE + x


def at(y, x):
    return (y + SIDE) % SIDE * SIDE + (x + SIDE) % SIDE


def greet(me, far_rows):
    y, x = me // SIDE, me % SIDE
    beside = jnp.where(x % 2 == 0, x - 1, x + 1)
    peers = [at(y, x + 1), at(y, x - 1), at(y + 1, x), at(y - 1, x), at(y + 1, beside), at(y - 1, beside)]
    if far_rows:
        peers += [at(y + 2, x), at(y + 2, beside)]
    barrier = pltpu.get_barrier_semaphore()
    for peer in peers:
        pl.semaphore_signal(barrier, inc=1, device_id={"ctx": peer}, device_id_type=MESH)
    pl.semaphore_wait(barrier, len(peers))


def send(src, dst, send_sem, recv_sem, to):
    return pltpu.make_async_remote_copy(
        src_ref=src, dst_ref=dst, send_sem=send_sem, recv_sem=recv_sem, device_id={"ctx": to}, device_id_type=MESH)


def gather_kernel(k_ref, v_ref, q_ref, do_ref, o_ref, k_all, v_all, q_out, do_out, de_out,
                  do_v, o_v, de_ref, hold, kv_send, kv_recv, row_send, row_recv, hop_recv, on_send, own_sem):
    me = lax.axis_index("ctx")
    y, x = me // SIDE, me % SIDE
    fetch = [pltpu.make_async_copy(do_ref, do_v, own_sem.at[5]), pltpu.make_async_copy(o_ref, o_v, own_sem.at[6])]
    for c in fetch:
        c.start()
    greet(me, True)
    HALF = BLOCK // 2

    def block(which, i, half=None):
        first, size = (i * BLOCK, BLOCK) if half is None else (i * BLOCK + half * HALF, HALF)
        return (k_all, v_all)[which].at[pl.ds(pl.multiple_of(first, HALF), size)]

    sent = []

    def push(which, slot, owner, to, half=None, src=None):
        c = send(block(which, owner, half) if src is None else src, block(which, owner, half),
                 kv_send.at[which, slot], kv_recv.at[which, owner, 0 if half is None else half], to)
        c.start()
        sent.append(c)

    def arrived(which, owner, half=None):
        b = block(which, owner, half)
        send(b, b, kv_send.at[which, 0], kv_recv.at[which, owner, 0 if half is None else half], me).wait_recv()

    def place(which, first, second):
        return at(y + second, x + first) if which == 0 else at(y + first, x + second)

    own = [pltpu.make_async_copy(ref, block(w, me), own_sem.at[w]) for w, ref in ((0, k_ref), (1, v_ref))]
    for w, ref in ((0, k_ref), (1, v_ref)):
        push(w, 0, me, place(w, 1, 0), src=ref)
        push(w, 1, me, place(w, -1, 0), src=ref)
    for w, ref in ((0, k_ref), (1, v_ref)):
        push(w, 4, me, place(w, 0, 1), src=ref)
        push(w, 5, me, place(w, 0, -1), src=ref)
    for c in own:
        c.start()

    rows = ((q_ref, q_out), (do_ref, do_out), (de_ref, de_out))

    def row_copy(n, c, r, to):
        src, dst = rows[n]
        return send(src.at[c], dst.at[r], row_send.at[n, c], row_recv.at[n, r], to)

    def hop_copy(n, c, side, to):
        return send(rows[n][0].at[c], hold.at[n, side], row_send.at[n, c], hop_recv.at[n, side], to)

    def on_copy(n, side, r, to):
        return send(hold.at[n, side], rows[n][1].at[r], on_send.at[n, side], row_recv.at[n, r], to)

    def own_row(n, c, r):
        src, dst = rows[n]
        return pltpu.make_async_copy(src.at[c], dst.at[r], own_sem.at[2 + n])

    def send_rows():
        turn = 1 - 2 * (lax.axis_index("grp") % 2)
        for n in range(2):
            for side in range(2):
                c = 2 * ((y + 2) % SIDE) + side
                hop = at(y + 1, x) if side == 0 else at(y - 1, taker_of(me, c) % SIDE)
                hop_copy(n, c, side, hop).start()
            for dy, side in ((1, 0), (-1, 0), (0, 1), (1, 1), (-1, 1)):
                c = 2 * ((y + dy * turn + SIDE) % SIDE) + side
                row_copy(n, c, me // 2, taker_of(me, c)).start()
            own_row(n, 2 * y, me // 2).start()

    def send_deltas():
        for c in fetch:
            c.wait()
        ones = jnp.ones((8, HD), jnp.float32)

        def chunk(c, _):
            for h in range(GQA):
                lanes = slice(h * HD, (h + 1) * HD)
                prod = do_v[c, :, lanes].astype(jnp.float32) * o_v[c, :, lanes].astype(jnp.float32)
                de_ref[c, :, h * TP:(h + 1) * TP] = lax.dot_general(
                    ones, prod, (((1,), (1,)), ((), ())), precision=lax.Precision.HIGHEST, preferred_element_type=jnp.float32)
            return 0
        lax.fori_loop(0, CHUNKS, chunk, 0)
        for c in range(CHUNKS):
            to = taker_of(me, c)

            @pl.when(to != me)
            def _():
                row_copy(2, c, me // 2, to).start()

            @pl.when(to == me)
            def _():
                own_row(2, c, me // 2).start()

    def pass_on():
        for side in range(2):
            owner = at(y - 1, x) if side == 0 else at(y + 1, jnp.where(x % 2 == 1, x + 1, x - 1))
            to = at(y + 1, x) if side == 0 else at(y - 1, x)
            for n in range(2):
                hop_copy(n, 0, side, me).wait_recv()
                on_copy(n, side, owner // 2, to).start()

    send_rows()
    send_deltas()
    for w in (0, 1):
        b = place(w, -1, 0)
        arrived(w, b)
        push(w, 2, b, place(w, 1, 0), half=0)
        b = place(w, 1, 0)
        arrived(w, b)
        push(w, 3, b, place(w, -1, 0), half=1)
    for n, s in ((1, 1), (2, -1)):
        for w in (0, 1):
            b = place(w, s, 0)
            push(w, 4 + 4 * n, b, place(w, 0, 1))
            push(w, 5 + 4 * n, b, place(w, 0, -1))
    for w in (0, 1):
        b = place(w, 2, 0)
        arrived(w, b, 0)
        arrived(w, b, 1)
        push(w, 16, b, place(w, 0, 1))
        push(w, 17, b, place(w, 0, -1))
    pass_on()
    for n, s in ((0, 0), (1, 1), (2, -1), (3, 2)):
        for w in (0, 1):
            b = place(w, s, -1)
            arrived(w, b)
            push(w, 6 + 4 * n, b, place(w, 0, 1), half=0)
            b = place(w, s, 1)
            arrived(w, b)
            push(w, 7 + 4 * n, b, place(w, 0, -1), half=1)
    for n, s in ((0, 0), (1, 1), (2, -1), (3, 2)):
        for w in (0, 1):
            b = place(w, s, 2)
            arrived(w, b, 0)
            arrived(w, b, 1)

    for r in range(CHUNKS):
        source, chunk = source_of(me, r)

        @pl.when(source != me)
        def _():
            for n in range(3):
                row_copy(n, 0, r, me).wait_recv()

        @pl.when(source == me)
        def _():
            for n in range(3):
                own_row(n, chunk, r).wait()

    for c in range(CHUNKS):
        @pl.when(taker_of(me, c) != me)
        def _():
            for n in range(3):
                row_copy(n, c, 0, me).wait_send()

    for side in range(2):
        for n in range(2):
            on_copy(n, side, 0, me).wait_send()
    for c in sent:
        c.wait_send()
    for c in own:
        c.wait()


def gather(k, v, q, do, o):
    anyspace = pl.BlockSpec(memory_space=pl.ANY)
    T = k.shape[0] * SENDERS
    sds = jax.ShapeDtypeStruct
    dma = pltpu.SemaphoreType.DMA
    de = (CHUNKS, 8, R)
    return pl.pallas_call(
        gather_kernel,
        out_shape=(sds((T, HD), k.dtype), sds((T, HD), k.dtype), sds(q.shape, q.dtype), sds(do.shape, do.dtype), sds(de, jnp.float32)),
        in_specs=[anyspace] * 5, out_specs=(anyspace,) * 5,
        scratch_shapes=[pltpu.VMEM(do.shape, do.dtype), pltpu.VMEM(o.shape, o.dtype), pltpu.VMEM(de, jnp.float32),
            pltpu.VMEM((2, 2) + q.shape[1:], q.dtype), dma((2, 20)), dma((2, SENDERS, 2)), dma((3, CHUNKS)), dma((3, CHUNKS)),
            dma((2, 2)), dma((2, 2)), dma((7,))],
        compiler_params=pltpu.CompilerParams(collective_id=0, has_side_effects=True, vmem_limit_bytes=60 * 2**20),
    )(k, v, q, do, o)


def reduce_kernel(dk_ref, dv_ref, dq_ref, dk_out, dv_out, dq_out, own, near, via, got, mid, via2, got2, hold,
                  send1, recv1, send2, recv2, row_send, row_recv, hop_recv, on_send, own_sem):
    me = lax.axis_index("ctx")
    y, x = me // SIDE, me % SIDE
    greet(me, False)
    HALF = BLOCK // 2
    refs = (dk_ref, dv_ref)
    outs = (dk_out, dv_out)
    sent = []

    def lane(w, leg):
        return (y, x)[(w + leg) % 2]

    def peer(w, leg, s):
        return at(y + s, x) if (w + leg) % 2 == 0 else at(y, x + s)

    def part(w, s, half):
        line = (lane(w, 0) + s + SIDE) % SIDE
        two = pl.ds(2 * half, 2)
        return refs[w].at[line, two] if w == 0 else refs[w].at[two, line]

    def push(src, dst, ssem, rsem, to):
        c = send(src, dst, ssem, rsem, to)
        c.start()
        sent.append(c)

    for w in (0, 1):
        up, down = peer(w, 0, 1), peer(w, 0, -1)
        push(part(w, 2, 0), via.at[w, 0], send1.at[w, 0], recv1.at[w, 0], up)
        push(part(w, 2, 1), via.at[w, 1], send1.at[w, 1], recv1.at[w, 1], down)
    for w in (0, 1):
        up, down = peer(w, 0, 1), peer(w, 0, -1)
        push(part(w, 1, 1), got.at[w, 0, 1], send1.at[w, 3], recv1.at[w, 3], up)
        push(part(w, -1, 0), got.at[w, 1, 0], send1.at[w, 4], recv1.at[w, 4], down)

    local = []
    for w in (0, 1):
        line = lane(w, 0)
        local.append(pltpu.make_async_copy(refs[w].at[line] if w == 0 else refs[w].at[:, line], own.at[w], own_sem.at[1 + 3 * w]))
        for d in (0, 1):
            local.append(pltpu.make_async_copy(part(w, 1 - 2 * d, d), near.at[w, d], own_sem.at[2 + 3 * w + d]))
    for c in local:
        c.start()

    def row_copy(r, c, to):
        return send(dq_ref.at[r], dq_out.at[c], row_send.at[r], row_recv.at[c], to)

    def hop_copy(r, side, to):
        return send(dq_ref.at[r], hold.at[side], row_send.at[r], hop_recv.at[side], to)

    def on_copy(side, c, to):
        return send(hold.at[side], dq_out.at[c], on_send.at[side], row_recv.at[c], to)

    def own_row(r, c):
        return pltpu.make_async_copy(dq_ref.at[r], dq_out.at[c], own_sem.at[0])

    def send_rows():
        turn = 1 - 2 * (lax.axis_index("grp") % 2)
        for dy, odd in ((2, 0), (2, 1), (1, 0), (-1, 0), (0, 0), (1, 1), (-1, 1), (0, 1)):
            r = 2 * ((y + dy * turn + SIDE) % SIDE) + odd
            to, c = source_of(me, r)
            if dy == 2:
                far = c % 2

                @pl.when(far == 0)
                def _():
                    hop_copy(r, 0, at(y + 1, x)).start()

                @pl.when(far == 1)
                def _():
                    hop_copy(r, 1, at(y - 1, to % SIDE)).start()
            elif dy == 0:
                @pl.when(to != me)
                def _():
                    row_copy(r, c, to).start()

                @pl.when(to == me)
                def _():
                    own_row(r, c).start()
            else:
                row_copy(r, c, to).start()

    def wait1(w, slot, dst):
        send(dst, dst, send1.at[w, slot], recv1.at[w, slot], me).wait_recv()

    def tile(i):
        return pl.ds(pl.multiple_of(i * 128, 128), 128)

    for w in (0, 1):
        for d in (0, 1):
            wait1(w, d, via.at[w, d])
            local[3 * w + 1 + d].wait()

            def add(i, _, w=w, d=d):
                r = tile(i)
                for b in range(2):
                    mine = near[w, d, b, r, :]
                    via[w, d, b, r, :] = (via[w, d, b, r, :].astype(jnp.float32) + mine.astype(jnp.float32)).astype(jnp.bfloat16)
                return 0
            lax.fori_loop(0, BLOCK // 128, add, 0)
            push(via.at[w, d], got.at[w, d, d], send1.at[w, 2 if d == 0 else 5], recv1.at[w, 2 if d == 0 else 5],
                 peer(w, 0, 1 if d == 0 else -1))

    send_rows()

    def pass_back():
        for side in range(2):
            owner = at(y + 1, x) if side == 0 else at(y - 1, x)
            taker = at(y - 1, x) if side == 0 else at(y + 1, jnp.where(x % 2 == 0, x - 1, x + 1))
            c = 2 * (taker // SIDE) + side
            hop_copy(0, side, me).wait_recv()
            on_copy(side, c, owner).start()

    for w in (0, 1):
        for slot, d, h in ((3, 0, 1), (4, 1, 0), (2, 0, 0), (5, 1, 1)):
            wait1(w, slot, got.at[w, d, h])
        local[3 * w].wait()

        def add4(i, _, w=w):
            r = tile(i)
            for b in range(SIDE):
                mine = own[w, b, r, :]
                total = mine.astype(jnp.float32) + got[w, 0, b // 2, b % 2, r, :].astype(jnp.float32)
                mid[w, b, r, :] = (total + got[w, 1, b // 2, b % 2, r, :].astype(jnp.float32)).astype(jnp.bfloat16)
            return 0
        lax.fori_loop(0, BLOCK // 128, add4, 0)

        def half2(s, h, w=w):
            return mid.at[w, (lane(w, 1) + s + SIDE) % SIDE, pl.ds(h * HALF, HALF)]
        up, down = peer(w, 1, 1), peer(w, 1, -1)
        push(half2(2, 0), via2.at[w, 0], send2.at[w, 0], recv2.at[w, 0], up)
        push(half2(2, 1), via2.at[w, 1], send2.at[w, 1], recv2.at[w, 1], down)
        push(half2(1, 1), got2.at[w, 0, 1], send2.at[w, 3], recv2.at[w, 3], up)
        push(half2(-1, 0), got2.at[w, 1, 0], send2.at[w, 4], recv2.at[w, 4], down)

    pass_back()

    def wait2(w, slot, dst):
        send(dst, dst, send2.at[w, slot], recv2.at[w, slot], me).wait_recv()

    for w in (0, 1):
        for d in (0, 1):
            wait2(w, d, via2.at[w, d])
            line = (lane(w, 1) + (1 if d == 0 else 3)) % SIDE
            for i in range(2):
                r = pl.ds(i * 128, 128)
                mine = mid[w, line, pl.ds(d * HALF + i * 128, 128), :]
                via2[w, d, r, :] = (via2[w, d, r, :].astype(jnp.float32) + mine.astype(jnp.float32)).astype(jnp.bfloat16)
            push(via2.at[w, d], got2.at[w, d, d], send2.at[w, 2 if d == 0 else 5], recv2.at[w, 2 if d == 0 else 5],
                 peer(w, 1, 1 if d == 0 else -1))
    for w in (0, 1):
        for slot, d, h in ((3, 0, 1), (4, 1, 0), (2, 0, 0), (5, 1, 1)):
            wait2(w, slot, got2.at[w, d, h])
        for h in (0, 1):
            for i in range(2):
                r = pl.ds(i * 128, 128)
                out = pl.ds(h * HALF + i * 128, 128)
                total = mid[w, lane(w, 1), out, :].astype(jnp.float32) + got2[w, 0, h, r, :].astype(jnp.float32)
                outs[w][out, :] = (total + got2[w, 1, h, r, :].astype(jnp.float32)).astype(jnp.bfloat16)
    for c in range(CHUNKS):
        @pl.when(taker_of(me, c) != me)
        def _():
            row_copy(0, c, me).wait_recv()

        @pl.when(taker_of(me, c) == me)
        def _():
            own_row(me // 2, c).wait()

    for r in range(CHUNKS):
        @pl.when(source_of(me, r)[0] != me)
        def _():
            row_copy(r, 0, me).wait_send()

    for side in range(2):
        on_copy(side, 0, me).wait_send()
    for c in sent:
        c.wait_send()


def reduce(dk, dv, dq):
    anyspace = pl.BlockSpec(memory_space=pl.ANY)
    vm = pl.BlockSpec(memory_space=pltpu.VMEM)
    sds = jax.ShapeDtypeStruct
    dma = pltpu.SemaphoreType.DMA
    bf = jnp.bfloat16
    half = BLOCK // 2
    shape = (SIDE, SIDE, BLOCK, HD)
    return pl.pallas_call(
        reduce_kernel,
        out_shape=(sds((BLOCK, HD), bf), sds((BLOCK, HD), bf), sds(dq.shape, bf)),
        in_specs=[anyspace] * 3, out_specs=(vm, vm, anyspace),
        scratch_shapes=[pltpu.VMEM((2, SIDE, BLOCK, HD), bf), pltpu.VMEM((2, 2, 2, BLOCK, HD), bf),
            pltpu.VMEM((2, 2, 2, BLOCK, HD), bf), pltpu.VMEM((2, 2, 2, 2, BLOCK, HD), bf), pltpu.VMEM((2, SIDE, BLOCK, HD), bf),
            pltpu.VMEM((2, 2, half, HD), bf), pltpu.VMEM((2, 2, 2, half, HD), bf), pltpu.VMEM((2,) + dq.shape[1:], bf),
            dma((2, 6)), dma((2, 6)), dma((2, 6)), dma((2, 6)), dma((CHUNKS,)), dma((CHUNKS,)), dma((2,)), dma((2,)), dma((7,))],
        compiler_params=pltpu.CompilerParams(collective_id=1, has_side_effects=True, vmem_limit_bytes=60 * 2**20),
    )(dk.reshape(shape), dv.reshape(shape), dq)


def on_device(queries, attn_keys, attn_values, attn_output, output_grad, chain_lens):
    tiles = lambda a: a[0].reshape(CHUNKS, TP, -1)
    k, v, q, do, delta = gather(attn_keys[0], attn_values[0], tiles(queries), tiles(output_grad), tiles(attn_output))
    dq, dk, dv = call(chain_lens, q, do, delta, k, v)
    dk, dv, dq = reduce(dk, dv, dq)
    return dq.reshape(1, BLOCK, -1), dk[None], dv[None]


def solution(mesh):
    tok = P("grp", "ctx", None)
    return jax.shard_map(
        on_device,
        mesh=mesh,
        in_specs=(tok, tok, tok, tok, tok, P("grp", None)),
        out_specs=(tok, tok, tok),
        check_vma=False,
    )
```

```python
import functools, math
import jax, jax.numpy as jnp
from jax import lax
from jax.experimental import pallas as pl
from jax.experimental.pallas import tpu as pltpu
from jax.sharding import PartitionSpec as P

HD = 128
GQA = 8
BLOCK = 512
TP = 64
R = TP * GQA
SUB = 128
SB = 64
BIG = 1536
GCH = 256
SCALE = HD ** -0.5
STEP = 256
C2 = SCALE * math.log2(math.e)
NN = (((1,), (0,)), ((), ()))


def dot(a, b):
    return lax.dot_general(a, b, NN, preferred_element_type=jnp.float32)


def kernel(lens_ref, q_any, do_any, delta_ref, k_any, v_any, dq_any, dk_any, dv_any,
           kt, pbuf, mbuf, mrun, lrun, dka, dva, qs, dos, dqt, qst, dost, k_ref, q_ref, do_ref, v_ref, dq_ref, dk_ref, dv_ref, k_sem, in_sem, sem, out_sem):
    T = k_ref.shape[0]

    me = lax.axis_index("ctx")
    fetch = [pltpu.make_async_copy(src, dst, in_sem.at[n]) for n, (src, dst) in enumerate(((q_any, q_ref), (do_any, do_ref), (v_any, v_ref)))]

    def k_part(i):
        rows = pl.ds(pl.multiple_of(i * 512, 512), 512)
        return pltpu.make_async_copy(k_any.at[rows], k_ref.at[rows], k_sem.at[i])

    for i in range(T // 512):
        k_part(i).start()
    for c in fetch:
        c.start()

    def init(i, _):
        rows = pl.ds(pl.multiple_of(i * 512, 512), 512)
        k_part(i).wait()
        kt[:, rows] = k_ref[rows, :].T
        dka[rows, :] = jnp.zeros((512, HD), jnp.float32)
        dva[rows, :] = jnp.zeros((512, HD), jnp.float32)
        return 0
    lax.fori_loop(0, T // 512, init, 0)
    fetch[0].wait()
    fetch[1].wait()
    e0 = lens_ref[0, 0]
    e1 = e0 + lens_ref[0, 1]

    def dq_out(t):
        return pltpu.make_async_copy(dq_ref.at[t], dq_any.at[t], sem.at[t])

    def start_of(p):
        return jnp.where(p < e0, 0, jnp.where(p < e1, e0, e1))

    def tile(t, _):
        source, chunk = source_of(me, t)
        p0 = source * BLOCK + chunk * TP
        lo = (start_of(p0) // SUB) * SUB
        hi = ((p0 + TP + SUB - 1) // SUB) * SUB
        odd = (hi - lo) % STEP != 0
        hi = jnp.where(odd & (lo == 0), hi + SUB, hi)
        lo = jnp.where(odd & (lo > 0), lo - SUB, lo)
        nb = (hi - lo) // BIG
        rest = (hi - lo) - nb * BIG
        for h in range(GQA):
            qs[h * TP:(h + 1) * TP, :] = q_ref[t, :, h * HD:(h + 1) * HD]
            dos[h * TP:(h + 1) * TP, :] = do_ref[t, :, h * HD:(h + 1) * HD]
        qst[...] = qs[...].T
        dost[...] = dos[...].T
        rpos = p0 + lax.broadcasted_iota(jnp.int32, (1, R), 1) % TP
        rstart = start_of(rpos)
        last_start = start_of(p0 + TP - 1)

        def stats(first, size, masked):
            first = pl.multiple_of(first, SUB)
            s = dot(k_ref[pl.ds(first, size), :], qst[...])
            if masked:
                spos = first + lax.broadcasted_iota(jnp.int32, (size, 1), 0)
                s = jnp.where((spos >= rstart) & (spos <= rpos), s, -1e30)
            s = s.reshape(size // SB, SB // 8, 8, R)
            m = jnp.max(s, axis=1)
            p = jnp.exp2((s - m[:, None]) * C2)
            pbuf[pl.ds(first, size), :] = p.reshape(size, R)
            mbuf[pl.ds(first // SB, size // SB)] = m
            old = mrun[...]
            new = jnp.maximum(old, jnp.max(m, axis=0))
            lrun[...] = lrun[...] * jnp.exp2((old - new) * C2) + jnp.sum(jnp.sum(p, axis=1) * jnp.exp2((m - new) * C2), axis=0)
            mrun[...] = new

        def grads(first, size):
            first = pl.multiple_of(first, SUB)
            dss = []
            for c in range(size // GCH):
                here = pl.multiple_of(first + c * GCH, SUB)
                rows = pl.ds(here, GCH)
                f = jnp.exp2((mbuf[pl.ds(here // SB, GCH // SB)] - top) * C2) * linv
                p = (pbuf[rows, :].reshape(GCH // SB, SB // 8, 8, R) * f[:, None]).reshape(GCH, R)
                dp = dot(v_ref[rows, :], dost[...])
                dss.append((p * (dp - delta)).astype(jnp.bfloat16))
                dva[rows, :] += dot(p.astype(jnp.bfloat16), dos[...])
                dka[rows, :] += dot(dss[-1], qs[...])
            dqt[...] += dot(kt[:, pl.ds(first, size)], jnp.concatenate(dss, axis=0))

        def sweep(body, last):
            def big(j, _):
                body(lo + j * BIG, BIG)
                return 0
            lax.fori_loop(0, nb, big, 0)
            at = lo + nb * BIG
            for size in range(STEP, BIG, STEP):
                pl.when(rest == size)(functools.partial(last, at, size))

        def stats_any(first, size):
            need = (first < last_start) | (first + size - 1 > p0)
            pl.when(need)(lambda: stats(first, size, True))
            pl.when(jnp.logical_not(need))(lambda: stats(first, size, False))
        mrun[...] = jnp.full((8, R), -1e30, jnp.float32)
        lrun[...] = jnp.zeros((8, R), jnp.float32)
        sweep(stats_any, functools.partial(stats, masked=True))
        top = jnp.max(mrun[...], axis=0, keepdims=True)
        linv = 1.0 / jnp.sum(lrun[...] * jnp.exp2((mrun[...] - top) * C2), axis=0, keepdims=True)
        delta = delta_ref[t, 0:1, :]
        dqt[...] = jnp.zeros((HD, R), jnp.float32)
        pl.when(t == 0)(fetch[2].wait)
        sweep(grads, grads)
        dq = (dqt[...].T * SCALE).astype(jnp.bfloat16)
        for h in range(GQA):
            dq_ref[t, :, h * HD:(h + 1) * HD] = dq[h * TP:(h + 1) * TP, :]
        dq_out(t).start()
        return 0
    lax.fori_loop(0, q_ref.shape[0], tile, 0)

    def part_out(i, n):
        rows = pl.ds(pl.multiple_of(i * 1024, 1024), 1024)
        src, dst = ((dk_ref, dk_any), (dv_ref, dv_any))[n]
        return pltpu.make_async_copy(src.at[rows], dst.at[rows], out_sem.at[n, i])

    def fin(i, _):
        rows = pl.ds(pl.multiple_of(i * 1024, 1024), 1024)
        dk_ref[rows, :] = (dka[rows, :] * SCALE).astype(dk_ref.dtype)
        dv_ref[rows, :] = dva[rows, :].astype(dv_ref.dtype)
        part_out(i, 0).start()
        part_out(i, 1).start()
        return 0
    lax.fori_loop(0, T // 1024, fin, 0)

    def drain(i, _):
        part_out(i, 0).wait()
        part_out(i, 1).wait()
        return 0
    lax.fori_loop(0, T // 1024, drain, 0)

    def drain_q(t, _):
        dq_out(t).wait()
        return 0
    lax.fori_loop(0, q_ref.shape[0], drain_q, 0)


def call(lens, q, do, delta, k, v):
    T = k.shape[0]
    vm = pl.BlockSpec(memory_space=pltpu.VMEM)
    sm = pl.BlockSpec(memory_space=pltpu.SMEM)
    hbm = pl.BlockSpec(memory_space=pl.ANY)
    f32 = jnp.float32
    bf = jnp.bfloat16
    return pl.pallas_call(
        kernel,
        out_shape=(jax.ShapeDtypeStruct(q.shape, bf), jax.ShapeDtypeStruct((T, HD), bf), jax.ShapeDtypeStruct((T, HD), bf)),
        in_specs=[sm, hbm, hbm, vm, hbm, hbm],
        out_specs=(hbm, hbm, hbm),
        scratch_shapes=[pltpu.VMEM((HD, T), bf), pltpu.VMEM((T, R), f32), pltpu.VMEM((T // SB, 8, R), f32), pltpu.VMEM((8, R), f32), pltpu.VMEM((8, R), f32),
            pltpu.VMEM((T, HD), f32), pltpu.VMEM((T, HD), f32), pltpu.VMEM((R, HD), bf), pltpu.VMEM((R, HD), bf), pltpu.VMEM((HD, R), f32),
            pltpu.VMEM((HD, R), bf), pltpu.VMEM((HD, R), bf),
            pltpu.VMEM((T, HD), bf), pltpu.VMEM(q.shape, bf), pltpu.VMEM(q.shape, bf), pltpu.VMEM((T, HD), bf), pltpu.VMEM(q.shape, bf), pltpu.VMEM((T, HD), bf), pltpu.VMEM((T, HD), bf),
            pltpu.SemaphoreType.DMA((T // 512,)), pltpu.SemaphoreType.DMA((3,)), pltpu.SemaphoreType.DMA((q.shape[0],)), pltpu.SemaphoreType.DMA((2, T // 1024))],
        compiler_params=pltpu.CompilerParams(vmem_limit_bytes=60 * 2**20),
    )(lens, q, do, delta, k, v)


MESH = pl.DeviceIdType.MESH
SIDE = 4
SENDERS = SIDE * SIDE
CHUNKS = 8


def source_of(dev, r):
    y, x = dev // SIDE, dev % SIDE
    ahead = (x - 2 * (r % 2) + SIDE) % SIDE
    upper = jnp.where((ahead == 1) | (ahead == 2), 1, 0)
    far = jnp.where(ahead >= 2, 1, 0)
    return 2 * r + upper, 2 * y + far


def taker_of(owner, c):
    r, upper, far = owner // 2, owner % 2, c % 2
    x = (2 * (r % 2) + jnp.where(upper == 1, 1 + far, SIDE - far)) % SIDE
    return c // 2 * SIDE + x


def at(y, x):
    return (y + SIDE) % SIDE * SIDE + (x + SIDE) % SIDE


def greet(me, far_rows):
    y, x = me // SIDE, me % SIDE
    beside = jnp.where(x % 2 == 0, x - 1, x + 1)
    peers = [at(y, x + 1), at(y, x - 1), at(y + 1, x), at(y - 1, x), at(y + 1, beside), at(y - 1, beside)]
    if far_rows:
        peers += [at(y + 2, x), at(y + 2, beside)]
    barrier = pltpu.get_barrier_semaphore()
    for peer in peers:
        pl.semaphore_signal(barrier, inc=1, device_id={"ctx": peer}, device_id_type=MESH)
    pl.semaphore_wait(barrier, len(peers))


def send(src, dst, send_sem, recv_sem, to):
    return pltpu.make_async_remote_copy(
        src_ref=src, dst_ref=dst, send_sem=send_sem, recv_sem=recv_sem, device_id={"ctx": to}, device_id_type=MESH)


def gather_kernel(k_ref, v_ref, q_ref, do_ref, o_ref, k_all, v_all, q_out, do_out, de_out,
                  do_v, o_v, de_ref, hold, kv_send, kv_recv, row_send, row_recv, hop_recv, on_send, own_sem):
    me = lax.axis_index("ctx")
    y, x = me // SIDE, me % SIDE
    fetch = [pltpu.make_async_copy(do_ref, do_v, own_sem.at[5]), pltpu.make_async_copy(o_ref, o_v, own_sem.at[6])]
    for c in fetch:
        c.start()
    greet(me, True)
    HALF = BLOCK // 2

    def block(which, i, half=None):
        first, size = (i * BLOCK, BLOCK) if half is None else (i * BLOCK + half * HALF, HALF)
        return (k_all, v_all)[which].at[pl.ds(pl.multiple_of(first, HALF), size)]

    sent = []

    def push(which, slot, owner, to, half=None, src=None):
        c = send(block(which, owner, half) if src is None else src, block(which, owner, half),
                 kv_send.at[which, slot], kv_recv.at[which, owner, 0 if half is None else half], to)
        c.start()
        sent.append(c)

    def arrived(which, owner, half=None):
        b = block(which, owner, half)
        send(b, b, kv_send.at[which, 0], kv_recv.at[which, owner, 0 if half is None else half], me).wait_recv()

    def place(which, first, second):
        return at(y + second, x + first) if which == 0 else at(y + first, x + second)

    own = [pltpu.make_async_copy(ref, block(w, me), own_sem.at[w]) for w, ref in ((0, k_ref), (1, v_ref))]
    for w, ref in ((0, k_ref), (1, v_ref)):
        push(w, 0, me, place(w, 1, 0), src=ref)
        push(w, 1, me, place(w, -1, 0), src=ref)
    for w, ref in ((0, k_ref), (1, v_ref)):
        push(w, 4, me, place(w, 0, 1), src=ref)
        push(w, 5, me, place(w, 0, -1), src=ref)
    for c in own:
        c.start()

    rows = ((q_ref, q_out), (do_ref, do_out), (de_ref, de_out))

    def row_copy(n, c, r, to):
        src, dst = rows[n]
        return send(src.at[c], dst.at[r], row_send.at[n, c], row_recv.at[n, r], to)

    def hop_copy(n, c, side, to):
        return send(rows[n][0].at[c], hold.at[n, side], row_send.at[n, c], hop_recv.at[n, side], to)

    def on_copy(n, side, r, to):
        return send(hold.at[n, side], rows[n][1].at[r], on_send.at[n, side], row_recv.at[n, r], to)

    def own_row(n, c, r):
        src, dst = rows[n]
        return pltpu.make_async_copy(src.at[c], dst.at[r], own_sem.at[2 + n])

    def send_rows():
        turn = 1 - 2 * (lax.axis_index("grp") % 2)
        for n in range(2):
            for side in range(2):
                c = 2 * ((y + 2) % SIDE) + side
                hop = at(y + 1, x) if side == 0 else at(y - 1, taker_of(me, c) % SIDE)
                hop_copy(n, c, side, hop).start()
            for dy, side in ((1, 0), (-1, 0), (0, 1), (1, 1), (-1, 1)):
                c = 2 * ((y + dy * turn + SIDE) % SIDE) + side
                row_copy(n, c, me // 2, taker_of(me, c)).start()
            own_row(n, 2 * y, me // 2).start()

    def send_deltas():
        for c in fetch:
            c.wait()
        ones = jnp.ones((8, HD), jnp.float32)

        def chunk(c, _):
            for h in range(GQA):
                lanes = slice(h * HD, (h + 1) * HD)
                prod = do_v[c, :, lanes].astype(jnp.float32) * o_v[c, :, lanes].astype(jnp.float32)
                de_ref[c, :, h * TP:(h + 1) * TP] = lax.dot_general(
                    ones, prod, (((1,), (1,)), ((), ())), precision=lax.Precision.HIGHEST, preferred_element_type=jnp.float32)
            return 0
        lax.fori_loop(0, CHUNKS, chunk, 0)
        for c in range(CHUNKS):
            to = taker_of(me, c)

            @pl.when(to != me)
            def _():
                row_copy(2, c, me // 2, to).start()

            @pl.when(to == me)
            def _():
                own_row(2, c, me // 2).start()

    def pass_on():
        for side in range(2):
            owner = at(y - 1, x) if side == 0 else at(y + 1, jnp.where(x % 2 == 1, x + 1, x - 1))
            to = at(y + 1, x) if side == 0 else at(y - 1, x)
            for n in range(2):
                hop_copy(n, 0, side, me).wait_recv()
                on_copy(n, side, owner // 2, to).start()

    send_rows()
    send_deltas()
    for w in (0, 1):
        b = place(w, -1, 0)
        arrived(w, b)
        push(w, 2, b, place(w, 1, 0), half=0)
        b = place(w, 1, 0)
        arrived(w, b)
        push(w, 3, b, place(w, -1, 0), half=1)
    for n, s in ((1, 1), (2, -1)):
        for w in (0, 1):
            b = place(w, s, 0)
            push(w, 4 + 4 * n, b, place(w, 0, 1))
            push(w, 5 + 4 * n, b, place(w, 0, -1))
    for w in (0, 1):
        b = place(w, 2, 0)
        arrived(w, b, 0)
        arrived(w, b, 1)
        push(w, 16, b, place(w, 0, 1))
        push(w, 17, b, place(w, 0, -1))
    pass_on()
    for n, s in ((0, 0), (1, 1), (2, -1), (3, 2)):
        for w in (0, 1):
            b = place(w, s, -1)
            arrived(w, b)
            push(w, 6 + 4 * n, b, place(w, 0, 1), half=0)
            b = place(w, s, 1)
            arrived(w, b)
            push(w, 7 + 4 * n, b, place(w, 0, -1), half=1)
    for n, s in ((0, 0), (1, 1), (2, -1), (3, 2)):
        for w in (0, 1):
            b = place(w, s, 2)
            arrived(w, b, 0)
            arrived(w, b, 1)

    for r in range(CHUNKS):
        source, chunk = source_of(me, r)

        @pl.when(source != me)
        def _():
            for n in range(3):
                row_copy(n, 0, r, me).wait_recv()

        @pl.when(source == me)
        def _():
            for n in range(3):
                own_row(n, chunk, r).wait()

    for c in range(CHUNKS):
        @pl.when(taker_of(me, c) != me)
        def _():
            for n in range(3):
                row_copy(n, c, 0, me).wait_send()

    for side in range(2):
        for n in range(2):
            on_copy(n, side, 0, me).wait_send()
    for c in sent:
        c.wait_send()
    for c in own:
        c.wait()


def gather(k, v, q, do, o):
    anyspace = pl.BlockSpec(memory_space=pl.ANY)
    T = k.shape[0] * SENDERS
    sds = jax.ShapeDtypeStruct
    dma = pltpu.SemaphoreType.DMA
    de = (CHUNKS, 8, R)
    return pl.pallas_call(
        gather_kernel,
        out_shape=(sds((T, HD), k.dtype), sds((T, HD), k.dtype), sds(q.shape, q.dtype), sds(do.shape, do.dtype), sds(de, jnp.float32)),
        in_specs=[anyspace] * 5, out_specs=(anyspace,) * 5,
        scratch_shapes=[pltpu.VMEM(do.shape, do.dtype), pltpu.VMEM(o.shape, o.dtype), pltpu.VMEM(de, jnp.float32),
            pltpu.VMEM((2, 2) + q.shape[1:], q.dtype), dma((2, 20)), dma((2, SENDERS, 2)), dma((3, CHUNKS)), dma((3, CHUNKS)),
            dma((2, 2)), dma((2, 2)), dma((7,))],
        compiler_params=pltpu.CompilerParams(collective_id=0, has_side_effects=True, vmem_limit_bytes=60 * 2**20),
    )(k, v, q, do, o)


def reduce_kernel(dk_ref, dv_ref, dq_ref, dk_out, dv_out, dq_out, own, near, via, got, mid, via2, got2, hold,
                  send1, recv1, send2, recv2, row_send, row_recv, hop_recv, on_send, own_sem):
    me = lax.axis_index("ctx")
    y, x = me // SIDE, me % SIDE
    greet(me, False)
    HALF = BLOCK // 2
    refs = (dk_ref, dv_ref)
    outs = (dk_out, dv_out)
    sent = []

    def lane(w, leg):
        return (y, x)[(w + leg) % 2]

    def peer(w, leg, s):
        return at(y + s, x) if (w + leg) % 2 == 0 else at(y, x + s)

    def part(w, s, half):
        line = (lane(w, 0) + s + SIDE) % SIDE
        two = pl.ds(2 * half, 2)
        return refs[w].at[line, two] if w == 0 else refs[w].at[two, line]

    def push(src, dst, ssem, rsem, to):
        c = send(src, dst, ssem, rsem, to)
        c.start()
        sent.append(c)

    for w in (0, 1):
        up, down = peer(w, 0, 1), peer(w, 0, -1)
        push(part(w, 2, 0), via.at[w, 0], send1.at[w, 0], recv1.at[w, 0], up)
        push(part(w, 2, 1), via.at[w, 1], send1.at[w, 1], recv1.at[w, 1], down)
    for w in (0, 1):
        up, down = peer(w, 0, 1), peer(w, 0, -1)
        push(part(w, 1, 1), got.at[w, 0, 1], send1.at[w, 3], recv1.at[w, 3], up)
        push(part(w, -1, 0), got.at[w, 1, 0], send1.at[w, 4], recv1.at[w, 4], down)

    local = []
    for w in (0, 1):
        line = lane(w, 0)
        local.append(pltpu.make_async_copy(refs[w].at[line] if w == 0 else refs[w].at[:, line], own.at[w], own_sem.at[1 + 3 * w]))
        for d in (0, 1):
            local.append(pltpu.make_async_copy(part(w, 1 - 2 * d, d), near.at[w, d], own_sem.at[2 + 3 * w + d]))
    for c in local:
        c.start()

    def row_copy(r, c, to):
        return send(dq_ref.at[r], dq_out.at[c], row_send.at[r], row_recv.at[c], to)

    def hop_copy(r, side, to):
        return send(dq_ref.at[r], hold.at[side], row_send.at[r], hop_recv.at[side], to)

    def on_copy(side, c, to):
        return send(hold.at[side], dq_out.at[c], on_send.at[side], row_recv.at[c], to)

    def own_row(r, c):
        return pltpu.make_async_copy(dq_ref.at[r], dq_out.at[c], own_sem.at[0])

    def send_rows():
        turn = 1 - 2 * (lax.axis_index("grp") % 2)
        for dy, odd in ((2, 0), (2, 1), (1, 0), (-1, 0), (0, 0), (1, 1), (-1, 1), (0, 1)):
            r = 2 * ((y + dy * turn + SIDE) % SIDE) + odd
            to, c = source_of(me, r)
            if dy == 2:
                far = c % 2

                @pl.when(far == 0)
                def _():
                    hop_copy(r, 0, at(y + 1, x)).start()

                @pl.when(far == 1)
                def _():
                    hop_copy(r, 1, at(y - 1, to % SIDE)).start()
            elif dy == 0:
                @pl.when(to != me)
                def _():
                    row_copy(r, c, to).start()

                @pl.when(to == me)
                def _():
                    own_row(r, c).start()
            else:
                row_copy(r, c, to).start()

    def wait1(w, slot, dst):
        send(dst, dst, send1.at[w, slot], recv1.at[w, slot], me).wait_recv()

    def tile(i):
        return pl.ds(pl.multiple_of(i * 128, 128), 128)

    for w in (0, 1):
        for d in (0, 1):
            wait1(w, d, via.at[w, d])
            local[3 * w + 1 + d].wait()

            def add(i, _, w=w, d=d):
                r = tile(i)
                for b in range(2):
                    mine = near[w, d, b, r, :]
                    via[w, d, b, r, :] = (via[w, d, b, r, :].astype(jnp.float32) + mine.astype(jnp.float32)).astype(jnp.bfloat16)
                return 0
            lax.fori_loop(0, BLOCK // 128, add, 0)
            push(via.at[w, d], got.at[w, d, d], send1.at[w, 2 if d == 0 else 5], recv1.at[w, 2 if d == 0 else 5],
                 peer(w, 0, 1 if d == 0 else -1))

    send_rows()

    def pass_back():
        for side in range(2):
            owner = at(y + 1, x) if side == 0 else at(y - 1, x)
            taker = at(y - 1, x) if side == 0 else at(y + 1, jnp.where(x % 2 == 0, x - 1, x + 1))
            c = 2 * (taker // SIDE) + side
            hop_copy(0, side, me).wait_recv()
            on_copy(side, c, owner).start()

    for w in (0, 1):
        for slot, d, h in ((3, 0, 1), (4, 1, 0), (2, 0, 0), (5, 1, 1)):
            wait1(w, slot, got.at[w, d, h])
        local[3 * w].wait()

        def add4(i, _, w=w):
            r = tile(i)
            for b in range(SIDE):
                mine = own[w, b, r, :]
                total = mine.astype(jnp.float32) + got[w, 0, b // 2, b % 2, r, :].astype(jnp.float32)
                mid[w, b, r, :] = (total + got[w, 1, b // 2, b % 2, r, :].astype(jnp.float32)).astype(jnp.bfloat16)
            return 0
        lax.fori_loop(0, BLOCK // 128, add4, 0)

        def half2(s, h, w=w):
            return mid.at[w, (lane(w, 1) + s + SIDE) % SIDE, pl.ds(h * HALF, HALF)]
        up, down = peer(w, 1, 1), peer(w, 1, -1)
        push(half2(2, 0), via2.at[w, 0], send2.at[w, 0], recv2.at[w, 0], up)
        push(half2(2, 1), via2.at[w, 1], send2.at[w, 1], recv2.at[w, 1], down)
        push(half2(1, 1), got2.at[w, 0, 1], send2.at[w, 3], recv2.at[w, 3], up)
        push(half2(-1, 0), got2.at[w, 1, 0], send2.at[w, 4], recv2.at[w, 4], down)

    pass_back()

    def wait2(w, slot, dst):
        send(dst, dst, send2.at[w, slot], recv2.at[w, slot], me).wait_recv()

    for w in (0, 1):
        for d in (0, 1):
            wait2(w, d, via2.at[w, d])
            line = (lane(w, 1) + (1 if d == 0 else 3)) % SIDE
            for i in range(2):
                r = pl.ds(i * 128, 128)
                mine = mid[w, line, pl.ds(d * HALF + i * 128, 128), :]
                via2[w, d, r, :] = (via2[w, d, r, :].astype(jnp.float32) + mine.astype(jnp.float32)).astype(jnp.bfloat16)
            push(via2.at[w, d], got2.at[w, d, d], send2.at[w, 2 if d == 0 else 5], recv2.at[w, 2 if d == 0 else 5],
                 peer(w, 1, 1 if d == 0 else -1))
    for w in (0, 1):
        for slot, d, h in ((3, 0, 1), (4, 1, 0), (2, 0, 0), (5, 1, 1)):
            wait2(w, slot, got2.at[w, d, h])
        for h in (0, 1):
            for i in range(2):
                r = pl.ds(i * 128, 128)
                out = pl.ds(h * HALF + i * 128, 128)
                total = mid[w, lane(w, 1), out, :].astype(jnp.float32) + got2[w, 0, h, r, :].astype(jnp.float32)
                outs[w][out, :] = (total + got2[w, 1, h, r, :].astype(jnp.float32)).astype(jnp.bfloat16)
    for c in range(CHUNKS):
        @pl.when(taker_of(me, c) != me)
        def _():
            row_copy(0, c, me).wait_recv()

        @pl.when(taker_of(me, c) == me)
        def _():
            own_row(me // 2, c).wait()

    for r in range(CHUNKS):
        @pl.when(source_of(me, r)[0] != me)
        def _():
            row_copy(r, 0, me).wait_send()

    for side in range(2):
        on_copy(side, 0, me).wait_send()
    for c in sent:
        c.wait_send()


def reduce(dk, dv, dq):
    anyspace = pl.BlockSpec(memory_space=pl.ANY)
    vm = pl.BlockSpec(memory_space=pltpu.VMEM)
    sds = jax.ShapeDtypeStruct
    dma = pltpu.SemaphoreType.DMA
    bf = jnp.bfloat16
    half = BLOCK // 2
    shape = (SIDE, SIDE, BLOCK, HD)
    return pl.pallas_call(
        reduce_kernel,
        out_shape=(sds((BLOCK, HD), bf), sds((BLOCK, HD), bf), sds(dq.shape, bf)),
        in_specs=[anyspace] * 3, out_specs=(vm, vm, anyspace),
        scratch_shapes=[pltpu.VMEM((2, SIDE, BLOCK, HD), bf), pltpu.VMEM((2, 2, 2, BLOCK, HD), bf),
            pltpu.VMEM((2, 2, 2, BLOCK, HD), bf), pltpu.VMEM((2, 2, 2, 2, BLOCK, HD), bf), pltpu.VMEM((2, SIDE, BLOCK, HD), bf),
            pltpu.VMEM((2, 2, half, HD), bf), pltpu.VMEM((2, 2, 2, half, HD), bf), pltpu.VMEM((2,) + dq.shape[1:], bf),
            dma((2, 6)), dma((2, 6)), dma((2, 6)), dma((2, 6)), dma((CHUNKS,)), dma((CHUNKS,)), dma((2,)), dma((2,)), dma((7,))],
        compiler_params=pltpu.CompilerParams(collective_id=1, has_side_effects=True, vmem_limit_bytes=60 * 2**20),
    )(dk.reshape(shape), dv.reshape(shape), dq)


def on_device(queries, attn_keys, attn_values, attn_output, output_grad, chain_lens):
    tiles = lambda a: a[0].reshape(CHUNKS, TP, -1)
    k, v, q, do, delta = gather(attn_keys[0], attn_values[0], tiles(queries), tiles(output_grad), tiles(attn_output))
    dq, dk, dv = call(chain_lens, q, do, delta, k, v)
    dk, dv, dq = reduce(dk, dv, dq)
    return dq.reshape(1, BLOCK, -1), dk[None], dv[None]


def solution(mesh):
    tok = P("grp", "ctx", None)
    return jax.shard_map(
        on_device,
        mesh=mesh,
        in_specs=(tok, tok, tok, tok, tok, P("grp", None)),
        out_specs=(tok, tok, tok),
        check_vma=False,
    )
```
